256 devices in a mesh: role: 2 (over core), gx: 16 (over y_hi, z), gy: 8 (over x, y_lo).
Axes of the slice: x: 4, y: 4 (y_hi: 2, y_lo: 2; y = y_hi * 2 + y_lo), z: 8, core: 2. Of those that a mesh axis runs over, the one named last changes fastest.
Arguments:
- state: float32 [2, 4, 16, 128, 1024], P('role', None, None, 'gx', 'gy'), may hold values from -4 to 4
- turbine_mask: int32 [16, 128, 1024], P(None, 'gx', 'gy'), may hold values 0 or 1
- sample_x: int32 [1024], P('gy'), may hold values from 0 to 127, as said below
- gust_start: int32 [1], replicated, may hold values from -40 to 0
- gust_level: int32 [1024], P('gy'), may hold values from 0 to 3
Outputs:
- new_state: float32 [2, 4, 16, 128, 1024], P('role', None, None, 'gx', 'gy')
The draws below stay inside these ranges and needn't reach their ends.
Inputs may be any that keep to these rules, and one draw needn't show every extreme that they name: `sample_x`: row y's sampling column lies among columns 8 * (y mod (16)) to 8 * (y mod (16)) + 7.
All inputs are finite; a program needn't handle non-finite values. No bound on the sum of `turbine_mask` on one device may be relied on, other than what follows from the above.
Results may differ from the reference program's by a relative error of at most 0.0001.
Values sent between devices are 32-bit elements; how exact they have to be, the bound alone decides.
No kernel may reach another device: no remote copies, remote signals or barrier semaphores. Data moves between devices by JAX's collectives and lax.ppermute only.
A program may use at most 64 MiB of HBM per device.

```python
import math
import jax
import jax.numpy as jnp
from jax import lax

CX = 8
NZ = 16
SWEEPS = 6
NX = 128
NY = 1024


def draw_sample_x(key, part):
    key = jax.random.fold_in(key, 5)
    rows = jnp.arange(NY)
    tiles = NX // CX
    place = rows % tiles
    offset = jax.random.randint(key, (NY,), 0, CX)
    offset = jnp.where(rows == 0, 0, offset)
    offset = jnp.where(rows == tiles - 1, CX - 1, offset)
    return (place * CX + offset).astype(jnp.int32)


def layered_theta(key, noise, bottom, top, rough_amp):
    rough_key, phase_key = jax.random.split(key)
    height = jnp.arange(NZ).astype(jnp.float32) / float(max(NZ - 1, 1))
    rough = jax.random.uniform(rough_key, (2, NZ), jnp.float32, -rough_amp, rough_amp)
    profile = bottom + (top - bottom) * height[None, :] + rough
    phase = jax.random.uniform(phase_key, (2, 2), jnp.float32, 0.0, 1.0)
    xs = jnp.arange(NX).astype(jnp.float32) / float(NX)
    ys = jnp.arange(NY).astype(jnp.float32) / float(NY)
    along_x = jnp.sin(2.0 * math.pi * (xs[None, :, None] + phase[:, 0, None, None]))
    along_y = jnp.cos(2.0 * math.pi * (ys[None, None, :] + phase[:, 1, None, None]))
    horiz = along_x + 0.5 * along_y
    theta = profile[:, :, None, None] + horiz[:, None, :, :] + 0.8 * noise
    return jnp.clip(theta, -4.0, 4.0)


def draw_state(key, part):
    key = jax.random.fold_in(key, 7)
    noise_key, theta_key = jax.random.split(key)
    shape = (2, 4, NZ, NX, NY)
    noise = jax.random.normal(noise_key, shape, jnp.float32)
    theta = layered_theta(theta_key, noise[:, 3], -1.5, 1.5, 0.6)
    velocity = jnp.clip(noise[:, :3], -4.0, 4.0)
    return jnp.concatenate([velocity, theta[:, None]], axis=1).astype(jnp.float32)


def plant(drawn, rng, least, largest):
    dims = drawn.shape
    spot = [jax.random.randint(jax.random.fold_in(rng, axis), (), 0, dims[axis]) for axis in range(len(dims))]
    drawn = drawn.at[tuple(spot)].set(least)
    longest = dims.index(max(dims))
    spot[longest] = (spot[longest] + 1) % dims[longest]
    return drawn.at[tuple(spot)].set(largest)


def setup_inputs(seed: int = 0) -> dict:
    keys = jax.random.split(jax.random.key(seed), 6)
    return {
        "state": draw_state(jax.random.fold_in(keys[5], 71), 0),
        "turbine_mask": plant((jax.random.randint(keys[1], (NZ, NX, NY), 0, 6) < 1).astype(jnp.int32), jax.random.fold_in(keys[1], 1), 0, 1),
        "sample_x": draw_sample_x(jax.random.fold_in(keys[5], 71), 0),
        "gust_start": jax.random.randint(keys[3], (1,), -40, 1).astype(jnp.int32),
        "gust_level": plant(jax.random.randint(keys[4], (NY,), 0, 4), jax.random.fold_in(keys[4], 1), 0, 3).astype(jnp.int32),
    }


DT = 0.25
SMAG = 0.1
BETA = 0.5
PRINV = 3.0
CDRAG = 1.0
RISE = 40.0
EPS = 1e-06
SECTION_C = (1.0 / 3.0, 0.5, 1.0)
SECTION_T = (0.0, 1.0 / 3.0, 0.5)

def extend_x(field, periodic, left_face, copy_right):
    if periodic:
        return jnp.concatenate([field[..., -1:, :], field, field[..., :1, :]], axis=-2)
    if copy_right:
        right_face = field[..., -1:, :]
    else:
        right_face = jnp.zeros_like(field[..., -1:, :])
    return jnp.concatenate([left_face[..., None, :], field, right_face], axis=-2)

def extend_y(field):
    return jnp.concatenate([field[..., -1:], field, field[..., :1]], axis=-1)

def tendencies(state_q, x_padded, y_padded, mean_theta, drag_field):
    wall = (jnp.arange(4) != 2).astype(state_q.dtype)[:, None, None, None]
    z_padded = jnp.concatenate([state_q[:, :1] * wall, state_q, state_q[:, -1:] * wall], axis=1)
    grad_x = (x_padded[:, :, 2:, :] - x_padded[:, :, :-2, :]) * 0.5
    grad_y = (y_padded[..., 2:] - y_padded[..., :-2]) * 0.5
    grad_z = (z_padded[:, 2:] - z_padded[:, :-2]) * 0.5
    laplace = x_padded[:, :, 2:, :] + x_padded[:, :, :-2, :] + y_padded[..., 2:] + y_padded[..., :-2] + z_padded[:, 2:] + z_padded[:, :-2] - 6.0 * state_q
    u_vel, v_vel, w_vel, theta = (state_q[0], state_q[1], state_q[2], state_q[3])
    carried = u_vel * grad_x + v_vel * grad_y + w_vel * grad_z
    shear_xy = 0.5 * (grad_y[0] + grad_x[1])
    shear_xz = 0.5 * (grad_z[0] + grad_x[2])
    shear_yz = 0.5 * (grad_z[1] + grad_y[2])
    strain = grad_x[0] * grad_x[0] + grad_y[1] * grad_y[1] + grad_z[2] * grad_z[2] + 2.0 * (shear_xy * shear_xy + shear_xz * shear_xz + shear_yz * shear_yz)
    eddy_visc = SMAG * jnp.sqrt(2.0 * strain + EPS)
    wind_speed = jnp.sqrt(u_vel * u_vel + v_vel * v_vel + EPS)
    resist = drag_field * wind_speed
    rate_u = eddy_visc * laplace[0] - carried[0] - resist * u_vel
    rate_v = eddy_visc * laplace[1] - carried[1] - resist * v_vel
    rate_w = eddy_visc * laplace[2] - carried[2] + BETA * (theta - mean_theta)
    rate_t = PRINV * eddy_visc * laplace[3] - carried[3]
    return jnp.stack([rate_u, rate_v, rate_w, rate_t])

def divergence(tentative, u_x, v_y):
    w_vel = tentative[2]
    w_pad = jnp.concatenate([jnp.zeros_like(w_vel[:1]), w_vel, jnp.zeros_like(w_vel[:1])], axis=0)
    return (u_x[:, 2:, :] - u_x[:, :-2, :]) * 0.5 + (v_y[..., 2:] - v_y[..., :-2]) * 0.5 + (w_pad[2:] - w_pad[:-2]) * 0.5

def jacobi_sweep(padded, source):
    centre = padded[:, 1:-1, 1:-1]
    z_pad = jnp.concatenate([centre[:1], centre, centre[-1:]], axis=0)
    neighbours = padded[:, 2:, 1:-1] + padded[:, :-2, 1:-1] + padded[:, 1:-1, 2:] + padded[:, 1:-1, :-2] + z_pad[2:] + z_pad[:-2]
    return (neighbours - source) / 6.0

def advance_section(current, start_q, section_step, periodic, inflow, drag_field):
    zero_face = jnp.zeros((current.shape[1], current.shape[3]), current.dtype)
    x_padded = extend_x(current, periodic, inflow, True)
    y_padded = extend_y(current)
    mean_theta = (lax.optimization_barrier(jnp.sum(current[3], axis=(1, 2))) / float(NX * NY))[:, None, None]
    tendency_now = tendencies(current, x_padded, y_padded, mean_theta, drag_field)
    tentative = start_q + section_step * tendency_now
    inflow_u = zero_face if periodic else inflow[0]
    u_x = extend_x(tentative[0], periodic, inflow_u, True)
    v_y = extend_y(tentative[1])
    source = divergence(tentative, u_x, v_y) / section_step
    pressure = jnp.zeros_like(source)
    for sweep_index in range(SWEEPS):
        pressure = jacobi_sweep(extend_y(extend_x(pressure, periodic, zero_face, False)), source)
    bordered = extend_y(extend_x(pressure, periodic, zero_face, False))
    grad_x = (bordered[:, 2:, 1:-1] - bordered[:, :-2, 1:-1]) * 0.5
    grad_y = (bordered[:, 1:-1, 2:] - bordered[:, 1:-1, :-2]) * 0.5
    z_pad = jnp.concatenate([pressure[:1], pressure, pressure[-1:]], axis=0)
    grad_z = (z_pad[2:] - z_pad[:-2]) * 0.5
    return jnp.stack([tentative[0] - section_step * grad_x, tentative[1] - section_step * grad_y, tentative[2] - section_step * grad_z, tentative[3]])

def reference(state, turbine_mask, sample_x, gust_start, gust_level):
    drag_field = CDRAG * turbine_mask.astype(jnp.float32)
    gust_amp = 1.5 + gust_level.astype(jnp.float32)
    start_step = gust_start[0].astype(jnp.float32)
    first_pre = state[0]
    first_suc = state[1]
    precursor = first_pre
    successor = first_suc
    sample_index = jnp.broadcast_to(sample_x.astype(jnp.int32)[None, None, None, :], (4, first_pre.shape[1], 1, first_pre.shape[3]))
    for section in range(3):
        section_step = SECTION_C[section] * DT
        rise_frac = jnp.clip((SECTION_T[section] - start_step) / RISE, 0.0, 1.0)
        gust_speed = gust_amp * 0.5 * (1.0 - jnp.cos(math.pi * rise_frac))
        inflow = jnp.take_along_axis(precursor, sample_index, axis=2)[:, :, 0, :]
        inflow = inflow.at[0].add(gust_speed[None, :])
        new_pre = advance_section(precursor, first_pre, section_step, True, None, 0.0)
        new_suc = advance_section(successor, first_suc, section_step, False, inflow, drag_field)
        precursor = new_pre
        successor = new_suc
    return jnp.stack([precursor, successor])
```

```python
import functools
import math

import jax
import jax.numpy as jnp
from jax import lax
from jax.experimental import pallas as pl
from jax.experimental.pallas import tpu as pltpu
from jax.sharding import PartitionSpec as P

SWEEPS = 6
DT = 0.25
SMAG = 0.1
BETA = 0.5
PRINV = 3.0
CDRAG = 1.0
RISE = 40.0
EPS = 1e-06
SECTION_C = (1.0 / 3.0, 0.5, 1.0)
SECTION_T = (0.0, 1.0 / 3.0, 0.5)

CX = 8
NZ = 16
NY = 128
EXT = 3 * CX
WIDE = 2 * NY
CELLS = 131072.0
SIXTH = 1.0 / 6.0


def lanes(n):
    return lax.broadcasted_iota(jnp.int32, (NZ, n), 1)


def levels(n):
    return lax.broadcasted_iota(jnp.int32, (NZ, n), 0)


def row_next(v):
    return pltpu.roll(v, v.shape[-1] - 1, axis=1)


def row_prev(v):
    return pltpu.roll(v, 1, axis=1)


def up(v, ghost=None):
    top = v if ghost is None else ghost
    return jnp.where(levels(v.shape[1]) == NZ - 1, top, pltpu.roll(v, NZ - 1, axis=0))


def down(v, ghost=None):
    base = v if ghost is None else ghost
    return jnp.where(levels(v.shape[1]) == 0, base, pltpu.roll(v, 1, axis=0))


def wall_table(mean, step, depth):
    source = -0.5 * BETA * (up(mean, 0.0) - down(mean, 0.0))
    press = [-SIXTH * source] * (depth + 1)
    for _ in range(SWEEPS - 1):
        fresh = []
        for d in range(depth + 1):
            after = press[min(d + 1, depth)]
            before = press[d - 1] if d else (0.0 if depth else press[0])
            mid = press[d]
            fresh.append((after + before + 2.0 * mid + up(mid) + down(mid) - source) * SIXTH)
        press = fresh
    d_u = []
    d_w = []
    for d in range(depth + 1):
        after = press[min(d + 1, depth)]
        before = press[d - 1] if d else (0.0 if depth else press[0])
        d_u.append((-0.5 * step) * (after - before))
        d_w.append(-step * (BETA * mean + 0.5 * (up(press[d]) - down(press[d]))))
    return d_u, d_w


def wall_spot(role, gx, j):
    pos = CX * gx - CX + j
    left = pos
    right = 16 * CX - 1 - pos
    spot = jnp.clip(jnp.minimum(left, right), 0, 7)
    spot = jnp.where(role == 0, 7, spot)
    sign = jnp.where(left <= right, 1.0, -1.0)
    return spot, sign


def means_of(sums_ref, role):
    pre = jnp.sum(sums_ref[0], axis=1, keepdims=True) * (1.0 / CELLS)
    suc = jnp.sum(sums_ref[1], axis=1, keepdims=True) * (1.0 / CELLS)
    own = jnp.where(role == 0, pre, suc)
    return jnp.broadcast_to(pre, (NZ, NY)), jnp.broadcast_to(own, (NZ, NY))


def fill_wall(cu, cw, own, step):
    d_u, d_w = wall_table(own, step, 6)
    for d in range(8):
        cu[d] = d_u[min(d, 6)]
        cw[d] = d_w[min(d, 6)]


def strip_lane(f, jj):
    return 64 * (f % 2) + CX * jj


def pack(strips, f, jj, cells):
    base = strip_lane(f, jj)
    turned = pltpu.roll(cells, base, axis=1) if base else cells
    lane = lanes(NY)
    first = (lane >= base) & (lane < base + 8)
    low = (base - 8) % NY
    last = (lane >= low) & (lane < low + 8)
    head, tail = strips[f // 2]
    strips[f // 2] = (jnp.where(first, turned, head), jnp.where(last, turned, tail))


def halo_lanes(head, tail, f, jj):
    shift = (-strip_lane(f, jj)) % NY
    if shift:
        head = pltpu.roll(head, shift, axis=1)
        tail = pltpu.roll(tail, shift, axis=1)
    lane = lanes(NY)
    return jnp.where(lane < 8, head, jnp.where(lane >= NY - 8, tail, 0.0))


def column_of(ref, f, jj):
    return ref[f, pl.ds(jj, NZ, stride=CX), :]


def sample_of(picked, f, jj, cells, offset):
    picked[f] = jnp.where(offset == jj, cells, picked[f])


def first_kernel(info, state, drag, offset, gust, strips_out, plane_out, sums_out):
    del info
    strips = [(jnp.zeros((NZ, NY), jnp.float32),) * 2 for _ in range(3)]
    off = jnp.broadcast_to(offset[...], (NZ, NY))
    picked = [jnp.zeros((NZ, NY), jnp.float32) for _ in range(4)]
    sums = jnp.zeros((NZ, NY), jnp.float32)
    for jj in range(CX):
        for f in range(4):
            cells = column_of(state, f, jj)
            pack(strips, f, jj, cells)
            sample_of(picked, f, jj, cells, off)
            if f == 3:
                sums = sums + cells
        pack(strips, 4, jj, drag[pl.ds(jj, NZ, stride=CX), :])
    for part in range(3):
        strips_out[0, part] = strips[part][0]
        strips_out[1, part] = strips[part][1]
    plane_out[0] = picked[0] + jnp.where(off < CX, gust[...], 0.0)
    for f in range(1, 4):
        plane_out[f] = picked[f]
    sums_out[...] = sums


def section_kernel(section, info, *refs):
    later = section > 0
    last = section == 2
    refs = list(refs)

    def take(n):
        out = refs[:n]
        del refs[:n]
        return out

    tiles0 = take(3)
    strips0 = take(3)
    drags = take(3)
    tiles, strips = (take(3), take(3)) if later else (tiles0, strips0)
    (plane, plane_after, plane_before) = take(3)
    if later:
        (sums_in,) = take(1)
    if not last:
        offset, gust = take(2)
    (new_out,) = take(1)
    if not last:
        strips_out, plane_out, sums_out = take(3)
    ext, tent, drag, press, src, face, cu, cw = refs

    role = info[0]
    gx = info[1]
    step = SECTION_C[section] * DT
    at_first = (role == 1) & (gx == 0)
    at_last = (role == 1) & (gx == 15)
    lane = lanes(NY)

    for f in range(4):
        face[f, :, :NY] = plane[f]
        face[f, :, NY:] = jnp.where(
            lane < 8, plane_after[f], jnp.where(lane >= NY - 8, plane_before[f], 0.0)
        )
    if later:
        prev_step = SECTION_C[section - 1] * DT
        pre_mean, own_mean = means_of(sums_in, role)
        fill_wall(cu, cw, own_mean, prev_step)
        _, (pre_w,) = wall_table(pre_mean, prev_step, 0)
        face[2, :, :NY] += pre_w
        face[2, :, NY:] += pre_w

    for side in range(3):
        for jj in range(CX):
            j = side * CX + jj
            if later:
                spot, sign = wall_spot(role, gx, j)
            for f in range(4):
                own = column_of(tiles[side], f, jj)
                halo = halo_lanes(strips[side][0, f // 2], strips[side][1, f // 2], f, jj)
                if later and f == 0:
                    more = cu[spot] * sign
                    own = own + more
                    halo = halo + more
                if later and f == 2:
                    more = cw[spot]
                    own = own + more
                    halo = halo + more
                ext[f, j, :, :NY] = own
                ext[f, j, :, NY:] = halo
            drag[j, :, :NY] = drags[side][pl.ds(jj, NZ, stride=CX), :]
            drag[j, :, NY:] = halo_lanes(strips0[side][0, 2], strips0[side][1, 2], 4, jj)
            if later:
                for f in range(3):
                    tent[f, j, :, :NY] = column_of(tiles0[side], f, jj)
                    tent[f, j, :, NY:] = halo_lanes(
                        strips0[side][0, f // 2], strips0[side][1, f // 2], f, jj
                    )

    @pl.when(at_first)
    def _():
        for f in range(4):
            ext[f, CX - 1] = face[f]

    @pl.when(at_last)
    def _():
        for f in range(4):
            ext[f, 2 * CX] = ext[f, 2 * CX - 1]

    def rate_column(j):
        mid = [ext[f, j] for f in range(3)]
        after = [ext[f, j + 1] for f in range(3)]
        before = [ext[f, j - 1] for f in range(3)]
        nxt = [row_next(m) for m in mid]
        prv = [row_prev(m) for m in mid]
        hi = [up(mid[0]), up(mid[1]), up(mid[2], 0.0)]
        lo = [down(mid[0]), down(mid[1]), down(mid[2], 0.0)]
        u, v, w = mid
        g_x = [(after[f] - before[f]) * 0.5 for f in range(3)]
        g_y = [(nxt[f] - prv[f]) * 0.5 for f in range(3)]
        g_z = [(hi[f] - lo[f]) * 0.5 for f in range(3)]
        a = g_y[0] + g_x[1]
        b = g_z[0] + g_x[2]
        e = g_z[1] + g_y[2]
        strain = g_x[0] * g_x[0] + g_y[1] * g_y[1] + g_z[2] * g_z[2] + 0.5 * (a * a + b * b + e * e)
        nu = SMAG * jnp.sqrt(2.0 * strain + EPS)
        resist = drag[j] * jnp.sqrt(u * u + v * v + EPS)
        rates = []
        for f in range(3):
            lap = after[f] + before[f] + nxt[f] + prv[f] + hi[f] + lo[f] - 6.0 * mid[f]
            rates.append(nu * lap - (u * g_x[f] + v * g_y[f] + w * g_z[f]))
        rates[0] = rates[0] - resist * u
        rates[1] = rates[1] - resist * v
        rates[2] = rates[2] + BETA * ext[3, j]
        base = tent if later else ext
        for f in range(3):
            tent[f, j] = base[f, j] + step * rates[f]
        return u, v, w, nu

    def heat_column(j, u, v, w, nu):
        mid = ext[3, j]
        after = ext[3, j + 1]
        before = ext[3, j - 1]
        nxt = row_next(mid)
        prv = row_prev(mid)
        hi = up(mid)
        lo = down(mid)
        g_x = (after - before) * 0.5
        g_y = (nxt - prv) * 0.5
        g_z = (hi - lo) * 0.5
        lap = after + before + nxt + prv + hi + lo - 6.0 * mid
        rate = PRINV * nu * lap - (u * g_x + v * g_y + w * g_z)
        return step * rate[:, :NY]

    def outer(j, carry):
        rate_column(j)
        return carry

    lax.fori_loop(1, CX, outer, 0)
    lax.fori_loop(2 * CX, EXT - 1, outer, 0)

    def inner(jj, carry):
        u, v, w, nu = rate_column(jj + CX)
        heat = heat_column(jj + CX, u, v, w, nu)
        src[jj, :, :NY] = heat
        return carry

    lax.fori_loop(0, CX, inner, 0)

    strips_new = [(jnp.zeros((NZ, NY), jnp.float32),) * 2 for _ in range(2)]
    picked = [jnp.zeros((NZ, NY), jnp.float32) for _ in range(4)]
    sums = jnp.zeros((NZ, NY), jnp.float32)
    if not last:
        off = jnp.broadcast_to(offset[...], (NZ, NY))

    def emit(f, jj, cells):
        new_out[f, pl.ds(jj, NZ, stride=CX), :] = cells
        if not last:
            pack(strips_new, f, jj, cells)
            sample_of(picked, f, jj, cells, off)

    for jj in range(CX):
        theta = column_of(tiles0[1], 3, jj) + src[jj, :, :NY]
        sums = sums + theta
        emit(3, jj, theta)

    @pl.when(at_first)
    def _():
        tent[0, CX - 1] = face[0]

    @pl.when(at_last)
    def _():
        tent[0, 2 * CX] = tent[0, 2 * CX - 1]

    low = jnp.where(at_first, CX, 0)
    high = jnp.where(at_last, 2 * CX - 1, EXT)

    def inside(j, v):
        if CX <= j < 2 * CX:
            return v
        return jnp.where((j >= low) & (j <= high), v, 0.0)

    for j in range(2, EXT - 2):
        v = tent[1, j]
        w = tent[2, j]
        div = tent[0, j + 1] - tent[0, j - 1] + row_next(v) - row_prev(v) + up(w, 0.0) - down(w, 0.0)
        scaled = div * (0.5 * SIXTH / step)
        src[j] = scaled
        press[0, j] = inside(j, -scaled)
    for sweep in range(1, SWEEPS):
        old = press.at[(sweep - 1) % 2]
        new = press.at[sweep % 2]
        for j in range(2 + sweep, EXT - 2 - sweep):
            mid = old[j]
            total = old[j + 1] + old[j - 1] + row_next(mid) + row_prev(mid) + up(mid) + down(mid)
            new[j] = inside(j, total * SIXTH - src[j])
    final = press.at[(SWEEPS - 1) % 2]
    half = 0.5 * step
    for jj in range(CX):
        j = CX + jj
        mid = final[j]
        own = mid[:, :NY]
        emit(0, jj, tent[0, j, :, :NY] - half * (final[j + 1, :, :NY] - final[j - 1, :, :NY]))
        emit(1, jj, tent[1, j, :, :NY] - half * (row_next(mid) - row_prev(mid))[:, :NY])
        emit(2, jj, tent[2, j, :, :NY] - half * (up(own) - down(own)))
    if not last:
        for part in range(2):
            strips_out[0, part] = strips_new[part][0]
            strips_out[1, part] = strips_new[part][1]
        plane_out[0] = picked[0] + jnp.where(off < CX, gust[...], 0.0)
        for f in range(1, 4):
            plane_out[f] = picked[f]
        sums_out[...] = sums


def last_kernel(info, state, sums_in, out, cu, cw):
    role = info[0]
    gx = info[1]
    _, own_mean = means_of(sums_in, role)
    fill_wall(cu, cw, own_mean, SECTION_C[2] * DT)
    for jj in range(CX):
        spot, sign = wall_spot(role, gx, CX + jj)
        rows = pl.ds(jj, NZ, stride=CX)
        out[0, rows, :] = state[0, rows, :] + cu[spot] * sign
        out[1, rows, :] = state[1, rows, :]
        out[2, rows, :] = state[2, rows, :] + cw[spot]
        out[3, rows, :] = state[3, rows, :]


VMEM = pl.BlockSpec(memory_space=pltpu.VMEM)
SMEM = pl.BlockSpec(memory_space=pltpu.SMEM)
TILE = jax.ShapeDtypeStruct((4, NZ * CX, NY), jnp.float32)
PLANE = jax.ShapeDtypeStruct((4, NZ, NY), jnp.float32)
SUMS = jax.ShapeDtypeStruct((NZ, NY), jnp.float32)


def strips_shape(parts):
    return jax.ShapeDtypeStruct((2, parts, NZ, NY), jnp.float32)


def call(body, name, args, outs, scratch=()):
    return pl.pallas_call(
        body,
        name=name,
        out_shape=outs,
        in_specs=[SMEM] + [VMEM] * (len(args) - 1),
        out_specs=jax.tree.map(lambda _: VMEM, outs),
        scratch_shapes=list(scratch),
        compiler_params=pltpu.CompilerParams(vmem_limit_bytes=48 * 1024 * 1024),
    )(*args)


def wide(*lead):
    return pltpu.VMEM((*lead, NZ, WIDE), jnp.float32)


WALL = [pltpu.VMEM((8, NZ, NY), jnp.float32)] * 2


def section_call(section, args):
    outs = [TILE]
    if section < 2:
        outs += [strips_shape(2), PLANE, SUMS]
    scratch = [wide(4, EXT), wide(3, EXT), wide(EXT), wide(2, EXT), wide(EXT), wide(4)] + WALL
    return call(functools.partial(section_kernel, section), f"section{section}", args, outs, scratch)


def ring(count, distance):
    return [(i, (i + distance) % count) for i in range(count)]


def around_x(cells, distance):
    return lax.ppermute(cells, "gx", ring(16, distance))


def around_y(cells, distance):
    return lax.ppermute(cells, "gy", ring(8, distance))


def halo(tile, strips):
    left = around_x(tile, 1)
    right = around_x(tile, -1)
    head = around_y(strips[0], -1)
    tail = around_y(strips[1], 1)
    own = jnp.stack([head, tail])
    return (left, tile, right), (around_x(own, 1), own, around_x(own, -1))


def gathered(plane):
    axes = ("role", "gx")
    first = plane * 0.0
    for m in range(4):
        first = first + lax.ppermute(plane, axes, [(4 * g + m, 16 + 4 * g) for g in range(4)])
    second = first
    for g in range(1, 4):
        second = second + lax.ppermute(first, axes, [(16 + 4 * g, 16)])
    axes = ("role", "gx", "gy")
    spot = [128 + y for y in range(8)]
    after = lax.ppermute(second, axes, [(spot[(y + 1) % 8], spot[y]) for y in range(8)])
    before = lax.ppermute(second, axes, [(spot[(y - 1) % 8], spot[y]) for y in range(8)])
    return second, after, before


def swapped(cells, axis, mask):
    return lax.ppermute(cells, axis, [(i, i ^ mask) for i in range(lax.axis_size(axis))])


def summed(sums, role):
    pair = jnp.where((jnp.arange(2) == role)[:, None, None], sums[None], 0.0)
    pair = pair + swapped(pair, "role", 1)
    for axis, masks in (("gx", (1, 2, 3)), ("gx", (4, 8, 12)), ("gy", (1, 2, 3)), ("gy", (4,))):
        pair = pair + sum(swapped(pair, axis, m) for m in masks)
    return pair


def per_device(state, turbine_mask, sample_x, gust_start, gust_level):
    role = lax.axis_index("role")
    gx = lax.axis_index("gx")
    info = jnp.stack([role, gx]).astype(jnp.int32)
    start = state.reshape(4, NZ * CX, NY)
    drag = jnp.where(role == 1, CDRAG * turbine_mask.astype(jnp.float32), 0.0)
    drag = drag.reshape(NZ * CX, NY)
    offset = sample_x - gx * CX
    offset = jnp.where((offset >= 0) & (offset < CX), offset, CX)[None, :].astype(jnp.int32)
    amp = 1.5 + gust_level.astype(jnp.float32)
    began = gust_start[0].astype(jnp.float32)
    gusts = []
    for section in range(3):
        rise = jnp.clip((SECTION_T[section] - began) / RISE, 0.0, 1.0)
        gusts.append((amp * 0.5 * (1.0 - jnp.cos(math.pi * rise)))[None, :])

    strips, plane, sums = call(
        first_kernel,
        "first",
        (info, start, drag, offset, gusts[0]),
        [strips_shape(3), PLANE, SUMS],
    )
    drags = (around_x(drag, 1), drag, around_x(drag, -1))
    tiles0, strips0 = halo(start, strips)
    planes = gathered(plane)
    total = summed(sums, role)
    tile, strips, plane, sums = section_call(
        0, (info, *tiles0, *strips0, *drags, *planes, offset, gusts[1])
    )
    tiles, strip3 = halo(tile, strips)
    planes = gathered(plane)
    tile, strips, plane, sums1 = section_call(
        1, (info, *tiles0, *strips0, *drags, *tiles, *strip3, *planes, total, offset, gusts[2])
    )
    total = summed(sums, role)
    tiles, strip3 = halo(tile, strips)
    planes = gathered(plane)
    (tile,) = section_call(2, (info, *tiles0, *strips0, *drags, *tiles, *strip3, *planes, total))
    total = summed(sums1, role)
    out = call(last_kernel, "last", (info, tile, total), TILE, WALL)
    return out.reshape(1, 4, NZ, CX, NY)


def solution(mesh):
    placed = (P("role", None, None, "gx", "gy"), P(None, "gx", "gy"), P("gy"), P(), P("gy"))
    return jax.shard_map(
        per_device,
        mesh=mesh,
        in_specs=placed,
        out_specs=P("role", None, None, "gx", "gy"),
        check_vma=False,
    )
```

```python
import functools
import math

import jax
import jax.numpy as jnp
from jax import lax
from jax.experimental import pallas as pl
from jax.experimental.pallas import tpu as pltpu
from jax.sharding import PartitionSpec as P

SWEEPS = 6
DT = 0.25
SMAG = 0.1
BETA = 0.5
PRINV = 3.0
CDRAG = 1.0
RISE = 40.0
EPS = 1e-06
SECTION_C = (1.0 / 3.0, 0.5, 1.0)
SECTION_T = (0.0, 1.0 / 3.0, 0.5)

NZ = 16
NX = 128
ROWS = 8
EXT = 3 * ROWS
BLOCKS = 16
CELLS = 131072.0
SIXTH = 1.0 / 6.0
FIELD = ROWS * NZ
DRAG_AT = 4 * FIELD


def lanes(rows=NZ):
    return lax.broadcasted_iota(jnp.int32, (rows, NX), 1)


def levels():
    return lax.broadcasted_iota(jnp.int32, (NZ, NX), 0)


def turn(v, shift, axis):
    return pltpu.roll(v, shift, axis=axis)


def up(v, ghost=None):
    return jnp.where(levels() == NZ - 1, v if ghost is None else ghost, turn(v, NZ - 1, 0))


def down(v, ghost=None):
    return jnp.where(levels() == 0, v if ghost is None else ghost, turn(v, 1, 0))


class Walls:
    def __init__(self, walled):
        lane = lanes()
        limit = jnp.where(walled, NX, -NX)
        self.first = lane == limit - NX
        self.last = lane == limit - 1

    def after(self, v):
        return jnp.where(self.last, v, turn(v, NX - 1, 1))

    def before(self, v, ghost):
        return jnp.where(self.first, ghost, turn(v, 1, 1))

    def p_after(self, v):
        return jnp.where(self.last, 0.0, turn(v, NX - 1, 1))

    def p_before(self, v):
        return jnp.where(self.first, 0.0, turn(v, 1, 1))


def mean_change(walls, mean, step):
    source = -0.5 * BETA * (up(mean, 0.0) - down(mean, 0.0))
    press = -SIXTH * source
    for _ in range(SWEEPS - 1):
        around = walls.p_after(press) + walls.p_before(press) + 2.0 * press
        press = (around + up(press) + down(press) - source) * SIXTH
    d_u = (-0.5 * step) * (walls.p_after(press) - walls.p_before(press))
    d_w = -step * (BETA * mean + 0.5 * (up(press) - down(press)))
    return d_u, d_w


def level_lanes(sums):
    spread = jnp.where(lanes() == levels(), jnp.broadcast_to(sums, (NZ, NX)), 0.0)
    return jnp.sum(spread, axis=0, keepdims=True)


def lane_means(row, start):
    spread = jnp.where(lanes() == levels() + start, jnp.broadcast_to(row, (NZ, NX)), 0.0)
    mean = jnp.sum(spread, axis=1, keepdims=True) * (1.0 / CELLS)
    return jnp.broadcast_to(mean, (NZ, NX))


def swap_blocks(v):
    row = levels()
    group = lanes() // 8
    for bit in (8, 4, 2, 1):
        row_set = (row & bit) != 0
        group_set = (group & bit) != 0
        from_low = turn(turn(v, NZ - bit, 0), 8 * bit, 1)
        from_high = turn(turn(v, bit, 0), NX - 8 * bit, 1)
        v = jnp.where(row_set == group_set, v, jnp.where(row_set, from_high, from_low))
    return v


def owner_of(block, flip):
    straight = block if block < 8 else 23 - block
    other = 15 - block if block < 8 else block - 8
    return jnp.where(flip == 0, straight, other)


def sampled(picked, f, r, cells, sample):
    shift = lax.rem(f * ROWS + r - sample[r] + 2 * NX, NX)
    return jnp.where(lanes() == f * ROWS + r, turn(cells, shift, 1), picked)


def with_gust(picked, gust):
    lane = lanes()
    for r in range(ROWS):
        picked = picked + jnp.where(lane == r, gust[r], 0.0)
    return picked


def pack_kernel(info, state, drag, out):
    flip = info[1]
    for f in range(5):
        flat = (state[f] if f < 4 else drag[...]).T
        for block in range(BLOCKS):
            out[owner_of(block, flip), f] = flat[ROWS * block : ROWS * (block + 1)]


def first_kernel(info, sample, gust, chunks, buf, plane, sums_out):
    del info
    picked = jnp.zeros((NZ, NX), jnp.float32)
    sums = jnp.zeros((NZ, NX), jnp.float32)
    for f in range(5):
        for r in range(ROWS):
            spot = f * ROWS + r
            cells = swap_blocks(chunks[pl.ds(spot, BLOCKS, stride=5 * ROWS), :])
            buf[spot * NZ : (spot + 1) * NZ, :] = cells
            if f < 4:
                picked = sampled(picked, f, r, cells, sample)
            if f == 3:
                sums = sums + cells
    picked = with_gust(picked, gust)
    plane[...] = picked
    buf[5 * FIELD :, :] = picked
    sums_out[...] = level_lanes(jnp.sum(sums, axis=1, keepdims=True))


def section_kernel(section, info, *refs):
    refs = list(refs)

    def take(n):
        out = refs[:n]
        del refs[:n]
        return out

    if section < 2:
        sample, gust = take(2)
    starts = take(3)
    bufs = take(3) if section else starts
    if section < 2 or section == 2:
        (sums_in,) = take(1)
    if section < 2:
        new_out, plane_out, sums_out = take(3)
    else:
        (chunks_out,) = take(1)
    ext, tent, press, src, face = refs

    role = info[0]
    step = SECTION_C[section] * DT
    walls = Walls(role == 1)
    plane_at = (4 if section else 5) * FIELD

    if section == 1:
        totals = jnp.concatenate(
            [
                jnp.sum(sums_in[: sums_in.shape[0] // 2], axis=0, keepdims=True),
                jnp.sum(sums_in[sums_in.shape[0] // 2 :], axis=0, keepdims=True),
            ]
        )
        own = jnp.where(role == 0, totals[:1], totals[1:])
        prev_step = SECTION_C[0] * DT
        d_u, d_w = mean_change(walls, lane_means(own, 0), prev_step)
        _, pre_w = mean_change(Walls(role < 0), lane_means(totals[:1], 0), prev_step)
        mean = lane_means(own, NZ)

    for side in range(3):
        plane = bufs[side][plane_at : plane_at + NZ, :]
        for r in range(ROWS):
            j = side * ROWS + r
            for f in range(4):
                at = (f * ROWS + r) * NZ
                cells = bufs[side][at : at + NZ, :]
                shift = (NX - (f * ROWS + r)) % NX
                ghost = turn(plane, shift, 1) if shift else plane
                if section == 1 and f == 0:
                    cells = cells + d_u
                if section == 1 and f == 2:
                    cells = cells + d_w
                    ghost = ghost + pre_w
                ext[f, j] = cells
                face[f, j] = ghost

    def rate_row(side, r):
        j = side * ROWS + r
        mid = [ext[f, j] for f in range(3)]
        nxt = [ext[f, j + 1] for f in range(3)]
        prv = [ext[f, j - 1] for f in range(3)]
        after = [walls.after(m) for m in mid]
        before = [walls.before(mid[f], face[f, j]) for f in range(3)]
        hi = [up(mid[0]), up(mid[1]), up(mid[2], 0.0)]
        lo = [down(mid[0]), down(mid[1]), down(mid[2], 0.0)]
        u, v, w = mid
        g_x = [(after[f] - before[f]) * 0.5 for f in range(3)]
        g_y = [(nxt[f] - prv[f]) * 0.5 for f in range(3)]
        g_z = [(hi[f] - lo[f]) * 0.5 for f in range(3)]
        a = g_y[0] + g_x[1]
        b = g_z[0] + g_x[2]
        e = g_z[1] + g_y[2]
        strain = g_x[0] * g_x[0] + g_y[1] * g_y[1] + g_z[2] * g_z[2] + 0.5 * (a * a + b * b + e * e)
        nu = SMAG * jnp.sqrt(2.0 * strain + EPS)
        at = pl.multiple_of(DRAG_AT + r * NZ, NZ)
        resist = starts[side][pl.ds(at, NZ), :] * jnp.sqrt(u * u + v * v + EPS)
        rates = []
        for f in range(3):
            lap = after[f] + before[f] + nxt[f] + prv[f] + hi[f] + lo[f] - 6.0 * mid[f]
            rates.append(nu * lap - (u * g_x[f] + v * g_y[f] + w * g_z[f]))
        rates[0] = rates[0] - resist * u
        rates[1] = rates[1] - resist * v
        theta = ext[3, j]
        rates[2] = rates[2] + BETA * (theta - mean if section == 1 else theta)
        for f in range(3):
            at = pl.multiple_of((f * ROWS + r) * NZ, NZ)
            tent[f, j] = starts[side][pl.ds(at, NZ), :] + step * rates[f]
        return u, v, w, nu, theta

    def heat_row(r, u, v, w, nu, mid):
        j = ROWS + r
        nxt = ext[3, j + 1]
        prv = ext[3, j - 1]
        after = walls.after(mid)
        before = walls.before(mid, face[3, j])
        hi = up(mid)
        lo = down(mid)
        g_x = (after - before) * 0.5
        g_y = (nxt - prv) * 0.5
        g_z = (hi - lo) * 0.5
        lap = after + before + nxt + prv + hi + lo - 6.0 * mid
        rate = PRINV * nu * lap - (u * g_x + v * g_y + w * g_z)
        at = pl.multiple_of((3 * ROWS + r) * NZ, NZ)
        tent[3, j] = starts[1][pl.ds(at, NZ), :] + step * rate

    def outer(side, r, carry):
        rate_row(side, r)
        return carry

    def inner(r, carry):
        heat_row(r, *rate_row(1, r))
        return carry

    lax.fori_loop(1, ROWS, functools.partial(outer, 0), 0)
    lax.fori_loop(0, ROWS, inner, 0)
    lax.fori_loop(0, ROWS - 1, functools.partial(outer, 2), 0)

    for j in range(2, EXT - 2):
        u = tent[0, j]
        w = tent[2, j]
        div = walls.after(u) - walls.before(u, face[0, j])
        div = div + (tent[1, j + 1] - tent[1, j - 1]) + (up(w, 0.0) - down(w, 0.0))
        scaled = div * (0.5 * SIXTH / step)
        src[j] = scaled
        press[0, j] = -scaled
    for sweep in range(1, SWEEPS):
        old = press.at[(sweep - 1) % 2]
        new = press.at[sweep % 2]
        for j in range(2 + sweep, EXT - 2 - sweep):
            mid = old[j]
            total = walls.p_after(mid) + walls.p_before(mid) + old[j + 1] + old[j - 1]
            total = total + up(mid) + down(mid)
            new[j] = total * SIXTH - src[j]
    final = press.at[(SWEEPS - 1) % 2]

    picked = jnp.zeros((NZ, NX), jnp.float32)
    sums = jnp.zeros((NZ, NX), jnp.float32)
    half = 0.5 * step
    for r in range(ROWS):
        j = ROWS + r
        mid = final[j]
        fresh = (
            tent[0, j] - half * (walls.p_after(mid) - walls.p_before(mid)),
            tent[1, j] - half * (final[j + 1] - final[j - 1]),
            tent[2, j] - half * (up(mid) - down(mid)),
            tent[3, j],
        )
        for f in range(4):
            spot = f * ROWS + r
            if section < 2:
                new_out[spot * NZ : (spot + 1) * NZ, :] = fresh[f]
                picked = sampled(picked, f, r, fresh[f], sample)
            else:
                chunks_out[pl.ds(spot, BLOCKS, stride=5 * ROWS), :] = swap_blocks(fresh[f])
        sums = sums + fresh[3]
    if section < 2:
        picked = with_gust(picked, gust)
        new_out[plane_at if section else 4 * FIELD :, :] = picked
        plane_out[...] = picked
        row = level_lanes(jnp.sum(sums, axis=1, keepdims=True))
        sums_out[...] = turn(row, NZ, 1) + sums_in[...] if section == 0 else row
    else:
        row = jnp.sum(sums_in[...], axis=0, keepdims=True)
        for block in range(BLOCKS):
            at = (block * 5 + 4) * ROWS
            chunks_out[at : at + ROWS, :] = jnp.broadcast_to(row, (ROWS, NX))


def last_kernel(info, chunks, out):
    role = info[0]
    flip = info[1]
    gx = info[2]
    row = chunks[0, 4, :1]
    for block in range(1, BLOCKS):
        row = row + chunks[block, 4, :1]
    changes = mean_change(Walls(role == 1), lane_means(row, 0), SECTION_C[2] * DT)
    shift = lax.rem(NX - ROWS * gx, NX)
    for f in range(4):
        flat = jnp.concatenate([chunks[owner_of(block, flip), f] for block in range(BLOCKS)])
        out[f] = flat.T
        if f in (0, 2):
            change = turn(changes[f // 2], shift, 1)
            for x in range(8):
                rows = pl.ds(x, NZ, stride=8)
                out[f, rows, :] += jnp.broadcast_to(change[:, x : x + 1], (NZ, NX))


VMEM = pl.BlockSpec(memory_space=pltpu.VMEM)
SMEM = pl.BlockSpec(memory_space=pltpu.SMEM)


def shape(*dims):
    return jax.ShapeDtypeStruct(dims, jnp.float32)


def call(body, name, small, args, outs, scratch=()):
    return pl.pallas_call(
        body,
        name=name,
        out_shape=outs,
        in_specs=[SMEM] * len(small) + [VMEM] * len(args),
        out_specs=[VMEM] * len(outs),
        scratch_shapes=list(scratch),
        compiler_params=pltpu.CompilerParams(vmem_limit_bytes=48 * 1024 * 1024),
    )(*small, *args)


def section_call(section, small, args):
    if section < 2:
        outs = [shape(4 * FIELD + NZ, NX), shape(NZ, NX), shape(1, NX)]
    else:
        outs = [shape(BLOCKS * 5 * ROWS, NX)]
    row = (NZ, NX)
    scratch = [(4, EXT), (4, EXT), (2, EXT), (EXT,), (4, EXT)]
    scratch = [pltpu.VMEM((*lead, *row), jnp.float32) for lead in scratch]
    body = functools.partial(section_kernel, section)
    return call(body, f"section{section}", small, args, outs, scratch)


def ring_order():
    order = []
    for gy in range(8):
        low = list(range(8))
        high = list(range(15, 7, -1))
        order += [gx * 8 + gy for gx in (low + high if gy % 2 == 0 else high + low)]
    return order


def around(cells, distance):
    order = ring_order()
    route = [(d, order[(i + distance) % len(order)]) for i, d in enumerate(order)]
    return lax.ppermute(cells, ("gx", "gy"), route)


def inflow_to(buf, plane):
    plane = lax.ppermute(plane, "role", [(0, 1)])
    return lax.dynamic_update_slice(buf, plane, (buf.shape[0] - NZ, 0))


def halo(buf):
    return around(buf, 1), buf, around(buf, -1)


def every(row, axes, count):
    return lax.all_to_all(jnp.broadcast_to(row[None], (count, 1, NX)), axes, 0, 0)[:, 0]


def per_device(state, turbine_mask, sample_x, gust_start, gust_level):
    role = lax.axis_index("role")
    gx = lax.axis_index("gx")
    flip = lax.axis_index("gy") % 2
    info = jnp.stack([role, flip, gx]).astype(jnp.int32)
    drag = jnp.where(role == 1, CDRAG * turbine_mask.astype(jnp.float32), 0.0)
    block = jnp.where(gx < 8, jnp.where(flip == 0, gx, gx + 8), jnp.where(flip == 0, 23 - gx, 15 - gx))
    sample = lax.dynamic_slice(sample_x, (block * ROWS,), (ROWS,)).astype(jnp.int32)
    level = lax.dynamic_slice(gust_level, (block * ROWS,), (ROWS,))
    amp = 1.5 + level.astype(jnp.float32)
    began = gust_start[0].astype(jnp.float32)
    gusts = []
    for section in range(3):
        rise = jnp.clip((SECTION_T[section] - began) / RISE, 0.0, 1.0)
        gusts.append(amp * 0.5 * (1.0 - jnp.cos(math.pi * rise)))

    args = (state.reshape(4, 128, 128), drag.reshape(128, 128))
    (chunks,) = call(pack_kernel, "pack", (info,), args, [shape(BLOCKS, 5, ROWS, NX)])
    chunks = lax.all_to_all(chunks, "gx", 0, 0)
    outs = [shape(5 * FIELD + NZ, NX), shape(NZ, NX), shape(1, NX)]
    args = (chunks.reshape(BLOCKS * 5 * ROWS, NX),)
    buf, plane, sums0 = call(first_kernel, "first", (info, sample, gusts[0]), args, outs)
    starts = halo(inflow_to(buf, plane))
    buf, plane, sums = section_call(0, (info, sample, gusts[1]), (*starts, sums0))
    bufs = halo(inflow_to(buf, plane))
    totals = every(sums, ("role", "gx", "gy"), 256)
    buf, plane, sums = section_call(1, (info, sample, gusts[2]), (*starts, *bufs, totals))
    bufs = halo(inflow_to(buf, plane))
    totals = every(sums, "gy", 8)
    (chunks,) = section_call(2, (info,), (*starts, *bufs, totals))
    chunks = lax.all_to_all(chunks.reshape(BLOCKS, 5, ROWS, NX), "gx", 0, 0)
    (out,) = call(last_kernel, "last", (info,), (chunks,), [shape(4, 128, 128)])
    return out.reshape(1, 4, NZ, 8, 128)


def solution(mesh):
    placed = (P("role", None, None, "gx", "gy"), P(None, "gx", "gy"), P("gy"), P(), P("gy"))
    return jax.shard_map(
        per_device,
        mesh=mesh,
        in_specs=placed,
        out_specs=P("role", None, None, "gx", "gy"),
        check_vma=False,
    )
```

```python
import functools
import math

import jax
import jax.numpy as jnp
from jax import lax
from jax.experimental import pallas as pl
from jax.experimental.pallas import tpu as pltpu
from jax.sharding import PartitionSpec as P

SWEEPS = 6
DT = 0.25
SMAG = 0.1
BETA = 0.5
PRINV = 3.0
CDRAG = 1.0
RISE = 40.0
EPS = 1e-06
SECTION_C = (1.0 / 3.0, 0.5, 1.0)
SECTION_T = (0.0, 1.0 / 3.0, 0.5)

NZ = 16
NX = 128
ROWS = 8
EXT = 3 * ROWS
BLOCKS = 16
CELLS = 131072.0
SIXTH = 1.0 / 6.0
FIELD = ROWS * NZ
DRAG_AT = 4 * FIELD


def lanes(rows=NZ):
    return lax.broadcasted_iota(jnp.int32, (rows, NX), 1)


def levels():
    return lax.broadcasted_iota(jnp.int32, (NZ, NX), 0)


def turn(v, shift, axis):
    return pltpu.roll(v, shift, axis=axis)


def up(v, ghost=None):
    return jnp.where(levels() == NZ - 1, v if ghost is None else ghost, turn(v, NZ - 1, 0))


def down(v, ghost=None):
    return jnp.where(levels() == 0, v if ghost is None else ghost, turn(v, 1, 0))


class Walls:
    def __init__(self, walled):
        lane = lanes()
        limit = jnp.where(walled, NX, -NX)
        self.first = lane == limit - NX
        self.last = lane == limit - 1

    def after(self, v):
        return jnp.where(self.last, v, turn(v, NX - 1, 1))

    def before(self, v, ghost):
        return jnp.where(self.first, ghost, turn(v, 1, 1))

    def p_after(self, v):
        return jnp.where(self.last, 0.0, turn(v, NX - 1, 1))

    def p_before(self, v):
        return jnp.where(self.first, 0.0, turn(v, 1, 1))


def mean_change(walls, mean, step):
    source = -0.5 * BETA * (up(mean, 0.0) - down(mean, 0.0))
    press = -SIXTH * source
    for _ in range(SWEEPS - 1):
        around = walls.p_after(press) + walls.p_before(press) + 2.0 * press
        press = (around + up(press) + down(press) - source) * SIXTH
    d_u = (-0.5 * step) * (walls.p_after(press) - walls.p_before(press))
    d_w = -step * (BETA * mean + 0.5 * (up(press) - down(press)))
    return d_u, d_w


def level_lanes(sums):
    spread = jnp.where(lanes() == levels(), jnp.broadcast_to(sums, (NZ, NX)), 0.0)
    return jnp.sum(spread, axis=0, keepdims=True)


def lane_means(row, start):
    spread = jnp.where(lanes() == levels() + start, jnp.broadcast_to(row, (NZ, NX)), 0.0)
    mean = jnp.sum(spread, axis=1, keepdims=True) * (1.0 / CELLS)
    return jnp.broadcast_to(mean, (NZ, NX))


def role_totals(rows, role):
    pre = jnp.sum(rows[:8], axis=0, keepdims=True)
    suc = jnp.sum(rows[8:], axis=0, keepdims=True)
    return pre, jnp.where(role == 0, pre, suc)


def skewed(tiles):
    group = lanes(ROWS) // 8
    tiles = [tiles[-i % BLOCKS] for i in range(BLOCKS)]
    for bit in (1, 2, 4, 8):
        moved = (group & bit) != 0
        tiles = [jnp.where(moved, tiles[(i - bit) % BLOCKS], tiles[i]) for i in range(BLOCKS)]
    return tiles


def turned(tile, groups):
    shift = 8 * groups % NX
    return turn(tile, shift, 1) if shift else tile


def owner_of(block, flip):
    straight = block if block < 8 else 23 - block
    other = (8 if block == 0 else 16 - block) if block < 8 else (block - 7) % 8
    return jnp.where(flip == 0, straight, other)


def sampled(picked, f, r, cells, sample):
    shift = lax.rem(f * ROWS + r - sample[r] + 2 * NX, NX)
    return jnp.where(lanes() == f * ROWS + r, turn(cells, shift, 1), picked)


def with_gust(picked, gust):
    lane = lanes()
    for r in range(ROWS):
        picked = picked + jnp.where(lane == r, gust[r], 0.0)
    return picked


def pack_kernel(info, state, drag, out):
    flip = info[1]
    for f in range(5):
        flat = (state[f] if f < 4 else drag[...]).T
        flat = turn(flat, ROWS * info[2], 1)
        for block in range(BLOCKS):
            out[owner_of(block, flip), f] = flat[ROWS * block : ROWS * (block + 1)]


def first_kernel(info, sample, gust, chunks, buf, plane, sums_out):
    del info
    picked = jnp.zeros((NZ, NX), jnp.float32)
    sums = jnp.zeros((NZ, NX), jnp.float32)
    for f in range(5):
        tiles = skewed([chunks[s, f] for s in range(BLOCKS)])
        for z in range(NZ):
            buf[pl.ds(f * FIELD + z, ROWS, stride=NZ), :] = turned(tiles[z], -z)
    for f in range(4):
        for r in range(ROWS):
            spot = f * ROWS + r
            cells = buf[spot * NZ : (spot + 1) * NZ, :]
            picked = sampled(picked, f, r, cells, sample)
            if f == 3:
                sums = sums + cells
    sums_out[...] = level_lanes(jnp.sum(sums, axis=1, keepdims=True))
    picked = with_gust(picked, gust)
    plane[...] = picked
    buf[5 * FIELD :, :] = picked


def section_kernel(section, info, *refs):
    refs = list(refs)

    def take(n):
        out = refs[:n]
        del refs[:n]
        return out

    if section < 2:
        sample, gust = take(2)
    starts = take(3)
    bufs = take(3) if section else starts
    (sums_in,) = take(1)
    if section < 2:
        new_out, plane_out, sums_out = take(3)
    else:
        (chunks_out,) = take(1)
    ext, tent, press, src, face, natural = refs

    role = info[0]
    step = SECTION_C[section] * DT
    walls = Walls(role == 1)
    plane_at = (4 if section else 5) * FIELD

    if section:
        if section == 1:
            row = jnp.sum(sums_in[...], axis=0, keepdims=True)
            pre = turn(row, NX - NZ, 1)
            own = jnp.where(role == 0, pre, turn(row, NX - 2 * NZ, 1))
            spot = 0
        else:
            pre, own = role_totals(sums_in, role)
            spot = NZ
        prev_step = SECTION_C[section - 1] * DT
        d_u, d_w = mean_change(walls, lane_means(own, spot), prev_step)
        _, pre_w = mean_change(Walls(role < 0), lane_means(pre, spot), prev_step)

    for side in range(3):
        plane = bufs[side][plane_at : plane_at + NZ, :]
        for r in range(ROWS):
            j = side * ROWS + r
            for f in range(4):
                at = (f * ROWS + r) * NZ
                cells = bufs[side][at : at + NZ, :]
                shift = (NX - (f * ROWS + r)) % NX
                ghost = turn(plane, shift, 1) if shift else plane
                if section and f == 0:
                    cells = cells + d_u
                if section and f == 2:
                    cells = cells + d_w
                    ghost = ghost + pre_w
                ext[f, j] = cells
                face[f, j] = ghost

    def rate_row(side, r):
        j = side * ROWS + r
        mid = [ext[f, j] for f in range(3)]
        nxt = [ext[f, j + 1] for f in range(3)]
        prv = [ext[f, j - 1] for f in range(3)]
        after = [walls.after(m) for m in mid]
        before = [walls.before(mid[f], face[f, j]) for f in range(3)]
        hi = [up(mid[0]), up(mid[1]), up(mid[2], 0.0)]
        lo = [down(mid[0]), down(mid[1]), down(mid[2], 0.0)]
        u, v, w = mid
        g_x = [(after[f] - before[f]) * 0.5 for f in range(3)]
        g_y = [(nxt[f] - prv[f]) * 0.5 for f in range(3)]
        g_z = [(hi[f] - lo[f]) * 0.5 for f in range(3)]
        a = g_y[0] + g_x[1]
        b = g_z[0] + g_x[2]
        e = g_z[1] + g_y[2]
        strain = g_x[0] * g_x[0] + g_y[1] * g_y[1] + g_z[2] * g_z[2] + 0.5 * (a * a + b * b + e * e)
        nu = SMAG * jnp.sqrt(2.0 * strain + EPS)
        at = pl.multiple_of(DRAG_AT + r * NZ, NZ)
        resist = starts[side][pl.ds(at, NZ), :] * jnp.sqrt(u * u + v * v + EPS)
        rates = []
        for f in range(3):
            lap = after[f] + before[f] + nxt[f] + prv[f] + hi[f] + lo[f] - 6.0 * mid[f]
            rates.append(nu * lap - (u * g_x[f] + v * g_y[f] + w * g_z[f]))
        rates[0] = rates[0] - resist * u
        rates[1] = rates[1] - resist * v
        theta = ext[3, j]
        rates[2] = rates[2] + BETA * theta
        for f in range(3):
            at = pl.multiple_of((f * ROWS + r) * NZ, NZ)
            tent[f, j] = starts[side][pl.ds(at, NZ), :] + step * rates[f]
        return u, v, w, nu, theta

    def heat_row(r, u, v, w, nu, mid):
        j = ROWS + r
        nxt = ext[3, j + 1]
        prv = ext[3, j - 1]
        after = walls.after(mid)
        before = walls.before(mid, face[3, j])
        hi = up(mid)
        lo = down(mid)
        g_x = (after - before) * 0.5
        g_y = (nxt - prv) * 0.5
        g_z = (hi - lo) * 0.5
        lap = after + before + nxt + prv + hi + lo - 6.0 * mid
        rate = PRINV * nu * lap - (u * g_x + v * g_y + w * g_z)
        at = pl.multiple_of((3 * ROWS + r) * NZ, NZ)
        tent[3, j] = starts[1][pl.ds(at, NZ), :] + step * rate

    def outer(side, r, carry):
        rate_row(side, r)
        return carry

    def inner(r, carry):
        heat_row(r, *rate_row(1, r))
        return carry

    lax.fori_loop(1, ROWS, functools.partial(outer, 0), 0, unroll=True)
    lax.fori_loop(0, ROWS, inner, 0, unroll=True)
    lax.fori_loop(0, ROWS - 1, functools.partial(outer, 2), 0, unroll=True)

    for j in range(2, EXT - 2):
        u = tent[0, j]
        w = tent[2, j]
        div = walls.after(u) - walls.before(u, face[0, j])
        div = div + (tent[1, j + 1] - tent[1, j - 1]) + (up(w, 0.0) - down(w, 0.0))
        scaled = div * (0.5 * SIXTH / step)
        src[j] = scaled
        press[0, j] = -scaled
    for sweep in range(1, SWEEPS):
        old = press.at[(sweep - 1) % 2]
        new = press.at[sweep % 2]
        for j in range(2 + sweep, EXT - 2 - sweep):
            mid = old[j]
            total = walls.p_after(mid) + walls.p_before(mid) + old[j + 1] + old[j - 1]
            total = total + up(mid) + down(mid)
            new[j] = total * SIXTH - src[j]
    final = press.at[(SWEEPS - 1) % 2]

    picked = jnp.zeros((NZ, NX), jnp.float32)
    sums = jnp.zeros((NZ, NX), jnp.float32)
    half = 0.5 * step
    for r in range(ROWS):
        j = ROWS + r
        mid = final[j]
        fresh = (
            tent[0, j] - half * (walls.p_after(mid) - walls.p_before(mid)),
            tent[1, j] - half * (final[j + 1] - final[j - 1]),
            tent[2, j] - half * (up(mid) - down(mid)),
            tent[3, j],
        )
        for f in range(4):
            spot = f * ROWS + r
            if section < 2:
                new_out[spot * NZ : (spot + 1) * NZ, :] = fresh[f]
                picked = sampled(picked, f, r, fresh[f], sample)
            else:
                natural[pl.ds(f * FIELD + r, NZ, stride=ROWS), :] = fresh[f]
        sums = sums + fresh[3]
    if section < 2:
        picked = with_gust(picked, gust)
        new_out[plane_at if section else 4 * FIELD :, :] = picked
        plane_out[...] = picked
        row = level_lanes(jnp.sum(sums, axis=1, keepdims=True))
        if section == 0:
            for part in range(2):
                rows = sums_in[8 * part : 8 * (part + 1)]
                row = row + turn(jnp.sum(rows, axis=0, keepdims=True), NZ * (part + 1), 1)
        else:
            kept = jnp.where(lanes(1) < NZ, jnp.sum(sums_in[...], axis=0, keepdims=True), 0.0)
            row = row + turn(kept, NZ, 1)
        sums_out[...] = row
    else:
        for f in range(4):
            tiles = []
            for z in range(NZ):
                at = f * FIELD + z * ROWS
                tiles.append(turned(natural[at : at + ROWS, :], z))
            tiles = skewed(tiles)
            for s in range(BLOCKS):
                chunks_out[s, f] = tiles[s]
        for s in range(BLOCKS):
            chunks_out[s, 4] = jnp.broadcast_to(own, (ROWS, NX))


def last_kernel(info, chunks, out):
    role = info[0]
    flip = info[1]
    gx = info[2]
    row = chunks[0, 4, :1]
    for block in range(1, BLOCKS):
        row = row + chunks[block, 4, :1]
    changes = mean_change(Walls(role == 1), lane_means(row, 0), SECTION_C[2] * DT)
    shift = lax.rem(NX - ROWS * gx, NX)
    for f in range(4):
        flat = jnp.concatenate([chunks[owner_of(block, flip), f] for block in range(BLOCKS)])
        out[f] = turn(flat, shift, 1).T
        if f in (0, 2):
            change = turn(changes[f // 2], shift, 1)
            for x in range(8):
                rows = pl.ds(x, NZ, stride=8)
                out[f, rows, :] += jnp.broadcast_to(change[:, x : x + 1], (NZ, NX))


VMEM = pl.BlockSpec(memory_space=pltpu.VMEM)
SMEM = pl.BlockSpec(memory_space=pltpu.SMEM)


def shape(*dims):
    return jax.ShapeDtypeStruct(dims, jnp.float32)


def call(body, name, small, args, outs, scratch=()):
    return pl.pallas_call(
        body,
        name=name,
        out_shape=outs,
        in_specs=[SMEM] * len(small) + [VMEM] * len(args),
        out_specs=[VMEM] * len(outs),
        scratch_shapes=list(scratch),
        compiler_params=pltpu.CompilerParams(vmem_limit_bytes=48 * 1024 * 1024),
    )(*small, *args)


def section_call(section, small, args):
    if section < 2:
        outs = [shape(4 * FIELD + NZ, NX), shape(NZ, NX), shape(1, NX)]
    else:
        outs = [shape(BLOCKS, 5, ROWS, NX)]
    row = (NZ, NX)
    scratch = [(4, EXT), (4, EXT), (2, EXT), (EXT,), (4, EXT)]
    scratch = [pltpu.VMEM((*lead, *row), jnp.float32) for lead in scratch]
    scratch.append(pltpu.VMEM((4 * FIELD, NX), jnp.float32))
    body = functools.partial(section_kernel, section)
    return call(body, f"section{section}", small, args, outs, scratch)


def ring_order():
    order = []
    for gy in range(8):
        even = [*range(8), *range(15, 7, -1)]
        odd = [8, *range(15, 8, -1), *range(1, 8), 0]
        order += [gx * 8 + gy for gx in (odd if gy % 2 else even)]
    return order


def around(cells, distance):
    order = ring_order()
    route = [(d, order[(i + distance) % len(order)]) for i, d in enumerate(order)]
    return lax.ppermute(cells, ("gx", "gy"), route)


def inflow_to(buf, plane):
    plane = lax.ppermute(plane, "role", [(0, 1)])
    return lax.dynamic_update_slice(buf, plane, (buf.shape[0] - NZ, 0))


def halo(buf):
    return around(buf, 1), buf, around(buf, -1)


def every(row, axes, count):
    return lax.all_to_all(jnp.broadcast_to(row[None], (count, 1, NX)), axes, 0, 0)[:, 0]


def per_device(state, turbine_mask, sample_x, gust_start, gust_level):
    role = lax.axis_index("role")
    gx = lax.axis_index("gx")
    flip = lax.axis_index("gy") % 2
    info = jnp.stack([role, flip, gx]).astype(jnp.int32)
    drag = jnp.where(role == 1, CDRAG * turbine_mask.astype(jnp.float32), 0.0)
    even = jnp.where(gx < 8, gx, 23 - gx)
    odd = jnp.where(gx < 8, 8 + (gx + 7) % 8, jnp.where(gx == 8, 0, 16 - gx))
    block = jnp.where(flip == 0, even, odd)
    sample = lax.dynamic_slice(sample_x, (block * ROWS,), (ROWS,)).astype(jnp.int32)
    level = lax.dynamic_slice(gust_level, (block * ROWS,), (ROWS,))
    amp = 1.5 + level.astype(jnp.float32)
    began = gust_start[0].astype(jnp.float32)
    gusts = []
    for section in range(3):
        rise = jnp.clip((SECTION_T[section] - began) / RISE, 0.0, 1.0)
        gusts.append(amp * 0.5 * (1.0 - jnp.cos(math.pi * rise)))

    args = (state.reshape(4, 128, 128), drag.reshape(128, 128))
    (chunks,) = call(pack_kernel, "pack", (info,), args, [shape(BLOCKS, 5, ROWS, NX)])
    chunks = lax.all_to_all(chunks, "gx", 0, 0)
    outs = [shape(5 * FIELD + NZ, NX), shape(NZ, NX), shape(1, NX)]
    args = (chunks,)
    buf, plane, sums = call(first_kernel, "first", (info, sample, gusts[0]), args, outs)
    starts = halo(inflow_to(buf, plane))
    totals = every(sums, ("role", "gy"), 16)
    buf, plane, sums = section_call(0, (info, sample, gusts[1]), (*starts, totals))
    bufs = halo(inflow_to(buf, plane))
    totals = every(sums, "gx", 16)
    buf, plane, sums = section_call(1, (info, sample, gusts[2]), (*starts, *bufs, totals))
    bufs = halo(inflow_to(buf, plane))
    totals = every(sums, ("role", "gy"), 16)
    (chunks,) = section_call(2, (info,), (*starts, *bufs, totals))
    chunks = lax.all_to_all(chunks, "gx", 0, 0)
    (out,) = call(last_kernel, "last", (info,), (chunks,), [shape(4, 128, 128)])
    return out.reshape(1, 4, NZ, 8, 128)


def solution(mesh):
    placed = (P("role", None, None, "gx", "gy"), P(None, "gx", "gy"), P("gy"), P(), P("gy"))
    return jax.shard_map(
        per_device,
        mesh=mesh,
        in_specs=placed,
        out_specs=P("role", None, None, "gx", "gy"),
        check_vma=False,
    )
```

```python
import functools
import math

import jax
import jax.numpy as jnp
from jax import lax
from jax.experimental import pallas as pl
from jax.experimental.pallas import tpu as pltpu
from jax.sharding import PartitionSpec as P

SWEEPS = 6
DT = 0.25
SMAG = 0.1
BETA = 0.5
PRINV = 3.0
CDRAG = 1.0
RISE = 40.0
EPS = 1e-06
SECTION_C = (1.0 / 3.0, 0.5, 1.0)
SECTION_T = (0.0, 1.0 / 3.0, 0.5)

NZ = 16
NX = 128
ROWS = 8
EXT = 3 * ROWS
BLOCKS = 16
CELLS = 131072.0
SIXTH = 1.0 / 6.0
FIELD = ROWS * NZ
DRAG_AT = 4 * FIELD


def lanes(rows=NZ):
    return lax.broadcasted_iota(jnp.int32, (rows, NX), 1)


def levels():
    return lax.broadcasted_iota(jnp.int32, (NZ, NX), 0)


def turn(v, shift, axis):
    return pltpu.roll(v, shift, axis=axis)


def up(v, ghost=None):
    low, high = v[:8], v[8:]
    edge = lax.broadcasted_iota(jnp.int32, (8, NX), 0) == 7
    low_up, high_up = turn(low, 7, 0), turn(high, 7, 0)
    top = jnp.where(edge, high if ghost is None else ghost, high_up)
    return jnp.concatenate([jnp.where(edge, high_up, low_up), top])


def down(v, ghost=None):
    low, high = v[:8], v[8:]
    edge = lax.broadcasted_iota(jnp.int32, (8, NX), 0) == 0
    low_down, high_down = turn(low, 1, 0), turn(high, 1, 0)
    base = jnp.where(edge, low if ghost is None else ghost, low_down)
    return jnp.concatenate([base, jnp.where(edge, low_down, high_down)])


def swap_blocks(v):
    row = levels()
    group = lanes() // 8
    for bit in (8, 4, 2, 1):
        row_set = (row & bit) != 0
        group_set = (group & bit) != 0
        from_low = turn(turn(v, NZ - bit, 0), 8 * bit, 1)
        from_high = turn(turn(v, bit, 0), NX - 8 * bit, 1)
        v = jnp.where(row_set == group_set, v, jnp.where(row_set, from_high, from_low))
    return v


class Walls:
    def __init__(self, walled):
        lane = lanes()
        limit = jnp.where(walled, NX, -NX)
        self.first = lane == limit - NX
        self.last = lane == limit - 1

    def after(self, v):
        return jnp.where(self.last, v, turn(v, NX - 1, 1))

    def before(self, v, ghost):
        return jnp.where(self.first, ghost, turn(v, 1, 1))

    def p_after(self, v):
        return jnp.where(self.last, 0.0, turn(v, NX - 1, 1))

    def p_before(self, v):
        return jnp.where(self.first, 0.0, turn(v, 1, 1))


def mean_change(walls, mean, step):
    source = -0.5 * BETA * (up(mean, 0.0) - down(mean, 0.0))
    press = -SIXTH * source
    for _ in range(SWEEPS - 1):
        around = walls.p_after(press) + walls.p_before(press) + 2.0 * press
        press = (around + up(press) + down(press) - source) * SIXTH
    d_u = (-0.5 * step) * (walls.p_after(press) - walls.p_before(press))
    d_w = -step * (BETA * mean + 0.5 * (up(press) - down(press)))
    return d_u, d_w


def level_lanes(sums):
    spread = jnp.where(lanes() == levels(), jnp.broadcast_to(sums, (NZ, NX)), 0.0)
    return jnp.sum(spread, axis=0, keepdims=True)


def lane_means(row, start, width=1):
    low = levels() * width + start
    lane = lanes()
    spread = jnp.where((lane >= low) & (lane < low + width), jnp.broadcast_to(row, (NZ, NX)), 0.0)
    mean = jnp.sum(spread, axis=1, keepdims=True) * (1.0 / CELLS)
    return jnp.broadcast_to(mean, (NZ, NX))


def role_totals(rows, role):
    half = rows.shape[0] // 2
    pre = jnp.sum(rows[:half], axis=0, keepdims=True)
    suc = jnp.sum(rows[half:], axis=0, keepdims=True)
    return pre, jnp.where(role == 0, pre, suc)


def skewed(tiles):
    group = lanes(ROWS) // 8
    tiles = [tiles[-i % BLOCKS] for i in range(BLOCKS)]
    for bit in (1, 2, 4, 8):
        moved = (group & bit) != 0
        tiles = [jnp.where(moved, tiles[(i - bit) % BLOCKS], tiles[i]) for i in range(BLOCKS)]
    return tiles


def turned(tile, groups):
    shift = 8 * groups % NX
    return turn(tile, shift, 1) if shift else tile


def owner_of(block, flip):
    straight = block if block < 8 else 23 - block
    other = (8 if block == 0 else 16 - block) if block < 8 else (block - 7) % 8
    return jnp.where(flip == 0, straight, other)


def sampled(picked, f, r, cells, sample):
    shift = lax.rem(f * ROWS + r - sample[r] + 2 * NX, NX)
    return jnp.where(lanes() == f * ROWS + r, turn(cells, shift, 1), picked)


def with_gust(picked, gust):
    lane = lanes()
    for r in range(ROWS):
        picked = picked + jnp.where(lane == r, gust[r], 0.0)
    return picked


def pack_kernel(info, state, mask, out):
    role = info[0]
    flip = info[1]
    for f in range(5):
        if f < 4:
            cells = state[f]
        else:
            cells = jnp.where(role == 1, CDRAG * mask[...].astype(jnp.float32), 0.0)
        flat = cells.T
        if f == 3:
            row = jnp.broadcast_to(jnp.sum(flat, axis=0, keepdims=True), (ROWS, NX))
            for block in range(BLOCKS):
                out[block, 5] = row
        flat = turn(flat, ROWS * info[2], 1)
        for block in range(BLOCKS):
            out[owner_of(block, flip), f] = flat[ROWS * block : ROWS * (block + 1)]


def first_kernel(info, sample, gust, chunks, buf, plane, sums_out):
    del info
    picked = jnp.zeros((NZ, NX), jnp.float32)
    sums = chunks[0, 5, :1]
    for s in range(1, BLOCKS):
        sums = sums + chunks[s, 5, :1]
    sums_out[...] = sums
    for f in range(5):
        tiles = skewed([chunks[s, f] for s in range(BLOCKS)])
        for z in range(NZ):
            buf[pl.ds(f * FIELD + z, ROWS, stride=NZ), :] = turned(tiles[z], -z)
    for f in range(4):
        for r in range(ROWS):
            spot = f * ROWS + r
            cells = buf[spot * NZ : (spot + 1) * NZ, :]
            picked = sampled(picked, f, r, cells, sample)
    picked = with_gust(picked, gust)
    plane[...] = picked
    buf[5 * FIELD :, :] = picked


def section_kernel(section, info, *refs):
    refs = list(refs)

    def take(n):
        out = refs[:n]
        del refs[:n]
        return out

    if section < 2:
        sample, gust = take(2)
    starts = take(3)
    bufs = take(3) if section else starts
    if section:
        (sums_in,) = take(1)
    if section < 2:
        new_out, plane_out, sums_out = take(3)
    else:
        (chunks_out,) = take(1)
    ext, tent, press, src, face, natural = refs

    role = info[0]
    step = SECTION_C[section] * DT
    walls = Walls(role == 1)
    plane_at = (4 if section else 5) * FIELD

    if section:
        pre, own = role_totals(sums_in, role)
        spot = (0, 8) if section == 1 else (NZ, 1)
        prev_step = SECTION_C[section - 1] * DT
        d_u, d_w = mean_change(walls, lane_means(own, *spot), prev_step)
        _, pre_w = mean_change(Walls(role < 0), lane_means(pre, *spot), prev_step)

    if section == 2:
        changes = mean_change(walls, lane_means(own * 0.5, 0), step)
        now_u, now_w = (swap_blocks(change) for change in changes)
        row = lax.broadcasted_iota(jnp.int32, (ROWS, NX), 0)
        for s in range(BLOCKS):
            share = jnp.where(row == 0, now_u[s : s + 1], now_w[s : s + 1])
            chunks_out[s, 4] = share

    for side in range(3):
        plane = bufs[side][plane_at : plane_at + NZ, :]
        for r in range(ROWS):
            j = side * ROWS + r
            for f in range(4):
                at = (f * ROWS + r) * NZ
                cells = bufs[side][at : at + NZ, :]
                shift = (NX - (f * ROWS + r)) % NX
                ghost = turn(plane, shift, 1) if shift else plane
                if section and f == 0:
                    cells = cells + d_u
                if section and f == 2:
                    cells = cells + d_w
                    ghost = ghost + pre_w
                ext[f, j] = cells
                face[f, j] = ghost

    def rate_row(side, r):
        j = side * ROWS + r
        mid = [ext[f, j] for f in range(3)]
        nxt = [ext[f, j + 1] for f in range(3)]
        prv = [ext[f, j - 1] for f in range(3)]
        after = [walls.after(m) for m in mid]
        before = [walls.before(mid[f], face[f, j]) for f in range(3)]
        hi = [up(mid[0]), up(mid[1]), up(mid[2], 0.0)]
        lo = [down(mid[0]), down(mid[1]), down(mid[2], 0.0)]
        u, v, w = mid
        g_x = [(after[f] - before[f]) * 0.5 for f in range(3)]
        g_y = [(nxt[f] - prv[f]) * 0.5 for f in range(3)]
        g_z = [(hi[f] - lo[f]) * 0.5 for f in range(3)]
        a = g_y[0] + g_x[1]
        b = g_z[0] + g_x[2]
        e = g_z[1] + g_y[2]
        strain = g_x[0] * g_x[0] + g_y[1] * g_y[1] + g_z[2] * g_z[2] + 0.5 * (a * a + b * b + e * e)
        nu = SMAG * jnp.sqrt(2.0 * strain + EPS)
        at = pl.multiple_of(DRAG_AT + r * NZ, NZ)
        resist = starts[side][pl.ds(at, NZ), :] * jnp.sqrt(u * u + v * v + EPS)
        rates = []
        for f in range(3):
            lap = after[f] + before[f] + nxt[f] + prv[f] + hi[f] + lo[f] - 6.0 * mid[f]
            rates.append(nu * lap - (u * g_x[f] + v * g_y[f] + w * g_z[f]))
        rates[0] = rates[0] - resist * u
        rates[1] = rates[1] - resist * v
        theta = ext[3, j]
        rates[2] = rates[2] + BETA * theta
        for f in range(3):
            at = pl.multiple_of((f * ROWS + r) * NZ, NZ)
            tent[f, j] = starts[side][pl.ds(at, NZ), :] + step * rates[f]
        return u, v, w, nu, theta

    def heat_row(r, u, v, w, nu, mid):
        j = ROWS + r
        nxt = ext[3, j + 1]
        prv = ext[3, j - 1]
        after = walls.after(mid)
        before = walls.before(mid, face[3, j])
        hi = up(mid)
        lo = down(mid)
        g_x = (after - before) * 0.5
        g_y = (nxt - prv) * 0.5
        g_z = (hi - lo) * 0.5
        lap = after + before + nxt + prv + hi + lo - 6.0 * mid
        rate = PRINV * nu * lap - (u * g_x + v * g_y + w * g_z)
        at = pl.multiple_of((3 * ROWS + r) * NZ, NZ)
        tent[3, j] = starts[1][pl.ds(at, NZ), :] + step * rate

    def outer(side, r, carry):
        rate_row(side, r)
        return carry

    def inner(r, carry):
        heat_row(r, *rate_row(1, r))
        return carry

    lax.fori_loop(1, ROWS, functools.partial(outer, 0), 0, unroll=True)
    lax.fori_loop(0, ROWS, inner, 0, unroll=True)
    lax.fori_loop(0, ROWS - 1, functools.partial(outer, 2), 0, unroll=True)

    for j in range(2, EXT - 2):
        u = tent[0, j]
        w = tent[2, j]
        div = walls.after(u) - walls.before(u, face[0, j])
        div = div + (tent[1, j + 1] - tent[1, j - 1]) + (up(w, 0.0) - down(w, 0.0))
        scaled = div * (0.5 * SIXTH / step)
        src[j] = scaled
        press[0, j] = -scaled
    for sweep in range(1, SWEEPS):
        old = press.at[(sweep - 1) % 2]
        new = press.at[sweep % 2]
        for j in range(2 + sweep, EXT - 2 - sweep):
            mid = old[j]
            total = walls.p_after(mid) + walls.p_before(mid) + old[j + 1] + old[j - 1]
            total = total + up(mid) + down(mid)
            new[j] = total * SIXTH - src[j]
    final = press.at[(SWEEPS - 1) % 2]

    picked = jnp.zeros((NZ, NX), jnp.float32)
    sums = jnp.zeros((NZ, NX), jnp.float32)
    half = 0.5 * step
    for r in range(ROWS):
        j = ROWS + r
        mid = final[j]
        fresh = (
            tent[0, j] - half * (walls.p_after(mid) - walls.p_before(mid)),
            tent[1, j] - half * (final[j + 1] - final[j - 1]),
            tent[2, j] - half * (up(mid) - down(mid)),
            tent[3, j],
        )
        for f in range(4):
            spot = f * ROWS + r
            if section < 2:
                new_out[spot * NZ : (spot + 1) * NZ, :] = fresh[f]
                picked = sampled(picked, f, r, fresh[f], sample)
            else:
                natural[pl.ds(f * FIELD + r, NZ, stride=ROWS), :] = fresh[f]
        sums = sums + fresh[3]
    if section < 2:
        picked = with_gust(picked, gust)
        new_out[plane_at if section else 4 * FIELD :, :] = picked
        plane_out[...] = picked
        sums_out[...] = level_lanes(jnp.sum(sums, axis=1, keepdims=True))
    else:
        for f in range(4):
            tiles = []
            for z in range(NZ):
                at = f * FIELD + z * ROWS
                tiles.append(turned(natural[at : at + ROWS, :], z))
            tiles = skewed(tiles)
            for s in range(BLOCKS):
                chunks_out[s, f] = tiles[s]


def last_kernel(info, chunks, out, held, left):
    flip = info[1]
    gx = info[2]
    share = chunks[0, 4]
    for block in range(1, BLOCKS):
        share = share + chunks[block, 4]
    shift = lax.rem(NX - ROWS * gx, NX)
    copies = [pltpu.make_async_copy(held.at[f], out.at[f], left.at[f]) for f in range(4)]
    for f in range(4):
        flat = jnp.concatenate([chunks[owner_of(block, flip), f] for block in range(BLOCKS)])
        flat = turn(flat, shift, 1)
        if f in (0, 2):
            flat = flat + share[f // 2 : f // 2 + 1]
        held[f] = flat.T
        copies[f].start()
    for copy in copies:
        copy.wait()


VMEM = pl.BlockSpec(memory_space=pltpu.VMEM)
SMEM = pl.BlockSpec(memory_space=pltpu.SMEM)
HBM = pl.BlockSpec(memory_space=pltpu.HBM)


def shape(*dims):
    return jax.ShapeDtypeStruct(dims, jnp.float32)


def call(body, name, small, args, outs, scratch=(), in_place=(VMEM, VMEM)):
    return pl.pallas_call(
        body,
        name=name,
        out_shape=outs,
        in_specs=[SMEM] * len(small) + [in_place[0]] * len(args),
        out_specs=[in_place[1]] * len(outs),
        scratch_shapes=list(scratch),
        compiler_params=pltpu.CompilerParams(vmem_limit_bytes=48 * 1024 * 1024),
    )(*small, *args)


def section_call(section, small, args):
    if section < 2:
        outs = [shape(4 * FIELD + NZ, NX), shape(NZ, NX), shape(1, NX)]
    else:
        outs = [shape(BLOCKS, 5, ROWS, NX)]
    row = (NZ, NX)
    scratch = [(4, EXT), (4, EXT), (2, EXT), (EXT,), (4, EXT)]
    scratch = [pltpu.VMEM((*lead, *row), jnp.float32) for lead in scratch]
    scratch.append(pltpu.VMEM((4 * FIELD, NX), jnp.float32))
    body = functools.partial(section_kernel, section)
    return call(body, f"section{section}", small, args, outs, scratch)


def ring_order():
    order = []
    for gy in range(8):
        even = [*range(8), *range(15, 7, -1)]
        odd = [8, *range(15, 8, -1), *range(1, 8), 0]
        order += [gx * 8 + gy for gx in (odd if gy % 2 else even)]
    return order


def around(cells, distance):
    order = ring_order()
    route = [(d, order[(i + distance) % len(order)]) for i, d in enumerate(order)]
    return lax.ppermute(cells, ("gx", "gy"), route)


def inflow_to(buf, plane):
    plane = lax.ppermute(plane, "role", [(0, 1)])
    return lax.dynamic_update_slice(buf, plane, (buf.shape[0] - NZ, 0))


def halo(buf):
    return around(buf, 1), buf, around(buf, -1)


def every(row, axes, count):
    return lax.all_to_all(jnp.broadcast_to(row[None], (count, 1, NX)), axes, 0, 0)[:, 0]


def along_z(row):
    groups = [list(range(8)), list(range(8, 16))]
    rows = jnp.broadcast_to(row[None], (8, 1, NX))
    return lax.all_to_all(rows, "gx", 0, 0, axis_index_groups=groups)[:, 0]


def across_z(row):
    high = [(role * 16 + half * 8) * 8 for role in range(2) for half in range(2)]
    groups = [[h + z * 8 + gy for h in high for gy in range(8)] for z in range(8)]
    rows = jnp.broadcast_to(row[None], (32, 1, NX))
    return lax.all_to_all(rows, ("role", "gx", "gy"), 0, 0, axis_index_groups=groups)[:, 0]


def per_device(state, turbine_mask, sample_x, gust_start, gust_level):
    role = lax.axis_index("role")
    gx = lax.axis_index("gx")
    flip = lax.axis_index("gy") % 2
    info = jnp.stack([role, flip, gx]).astype(jnp.int32)
    even = jnp.where(gx < 8, gx, 23 - gx)
    odd = jnp.where(gx < 8, 8 + (gx + 7) % 8, jnp.where(gx == 8, 0, 16 - gx))
    block = jnp.where(flip == 0, even, odd)
    sample = lax.dynamic_slice(sample_x, (block * ROWS,), (ROWS,)).astype(jnp.int32)
    level = lax.dynamic_slice(gust_level, (block * ROWS,), (ROWS,))
    amp = 1.5 + level.astype(jnp.float32)
    began = gust_start[0].astype(jnp.float32)
    gusts = []
    for section in range(3):
        rise = jnp.clip((SECTION_T[section] - began) / RISE, 0.0, 1.0)
        gusts.append(amp * 0.5 * (1.0 - jnp.cos(math.pi * rise)))

    args = (state.reshape(4, 128, 128), turbine_mask.reshape(128, 128))
    (chunks,) = call(pack_kernel, "pack", (info,), args, [shape(BLOCKS, 6, ROWS, NX)])
    chunks = lax.all_to_all(chunks, "gx", 0, 0)
    outs = [shape(5 * FIELD + NZ, NX), shape(NZ, NX), shape(1, NX)]
    args = (chunks,)
    buf, plane, sums = call(first_kernel, "first", (info, sample, gusts[0]), args, outs)
    starts = halo(inflow_to(buf, plane))
    totals = every(sums, ("role", "gy"), 16)
    buf, plane, sums = section_call(0, (info, sample, gusts[1]), starts)
    plane, totals = lax.optimization_barrier((plane, totals))
    bufs = halo(inflow_to(buf, plane))
    rows = along_z(sums)
    buf, plane, sums = section_call(1, (info, sample, gusts[2]), (*starts, *bufs, totals))
    plane, rows = lax.optimization_barrier((plane, rows))
    bufs = halo(inflow_to(buf, plane))
    row = jnp.sum(rows, axis=0, keepdims=True)
    row = jnp.concatenate([sums[:, :NZ], row[:, : NX - NZ]], axis=1)
    totals = across_z(row)
    (chunks,) = section_call(2, (info,), (*starts, *bufs, totals))
    chunks = lax.all_to_all(chunks, "gx", 0, 0)
    scratch = [pltpu.VMEM((4, 128, 128), jnp.float32), pltpu.SemaphoreType.DMA((4,))]
    outs = [shape(4, 128, 128)]
    (out,) = call(last_kernel, "last", (info,), (chunks,), outs, scratch, (VMEM, HBM))
    return out.reshape(1, 4, NZ, 8, 128)


def solution(mesh):
    placed = (P("role", None, None, "gx", "gy"), P(None, "gx", "gy"), P("gy"), P(), P("gy"))
    return jax.shard_map(
        per_device,
        mesh=mesh,
        in_specs=placed,
        out_specs=P("role", None, None, "gx", "gy"),
        check_vma=False,
    )
```

```python
import functools
import math

import jax
import jax.numpy as jnp
from jax import lax
from jax.experimental import pallas as pl
from jax.experimental.pallas import tpu as pltpu
from jax.sharding import PartitionSpec as P

SWEEPS = 6
DT = 0.25
SMAG = 0.1
BETA = 0.5
PRINV = 3.0
CDRAG = 1.0
RISE = 40.0
EPS = 1e-06
SECTION_C = (1.0 / 3.0, 0.5, 1.0)
SECTION_T = (0.0, 1.0 / 3.0, 0.5)

NZ = 16
NX = 128
ROWS = 8
EXT = 3 * ROWS
BLOCKS = 16
CELLS = 131072.0
SIXTH = 1.0 / 6.0
FIELD = ROWS * NZ
DRAG_AT = 4 * FIELD


def lanes(rows=NZ):
    return lax.broadcasted_iota(jnp.int32, (rows, NX), 1)


def levels():
    return lax.broadcasted_iota(jnp.int32, (NZ, NX), 0)


def turn(v, shift, axis):
    return pltpu.roll(v, shift, axis=axis)


def up(v, ghost=None):
    low, high = v[:8], v[8:]
    edge = lax.broadcasted_iota(jnp.int32, (8, NX), 0) == 7
    low_up, high_up = turn(low, 7, 0), turn(high, 7, 0)
    top = jnp.where(edge, high if ghost is None else ghost, high_up)
    return jnp.concatenate([jnp.where(edge, high_up, low_up), top])


def down(v, ghost=None):
    low, high = v[:8], v[8:]
    edge = lax.broadcasted_iota(jnp.int32, (8, NX), 0) == 0
    low_down, high_down = turn(low, 1, 0), turn(high, 1, 0)
    base = jnp.where(edge, low if ghost is None else ghost, low_down)
    return jnp.concatenate([base, jnp.where(edge, low_down, high_down)])


def swap_blocks(v):
    row = levels()
    group = lanes() // 8
    for bit in (8, 4, 2, 1):
        row_set = (row & bit) != 0
        group_set = (group & bit) != 0
        from_low = turn(turn(v, NZ - bit, 0), 8 * bit, 1)
        from_high = turn(turn(v, bit, 0), NX - 8 * bit, 1)
        v = jnp.where(row_set == group_set, v, jnp.where(row_set, from_high, from_low))
    return v


class Walls:
    def __init__(self, walled):
        lane = lanes()
        limit = jnp.where(walled, NX, -NX)
        self.first = lane == limit - NX
        self.last = lane == limit - 1

    def after(self, v):
        return jnp.where(self.last, v, turn(v, NX - 1, 1))

    def before(self, v, ghost):
        return jnp.where(self.first, ghost, turn(v, 1, 1))

    def p_after(self, v):
        return jnp.where(self.last, 0.0, turn(v, NX - 1, 1))

    def p_before(self, v):
        return jnp.where(self.first, 0.0, turn(v, 1, 1))


def mean_change(walls, mean, step):
    source = -0.5 * BETA * (up(mean, 0.0) - down(mean, 0.0))
    press = -SIXTH * source
    for _ in range(SWEEPS - 1):
        around = walls.p_after(press) + walls.p_before(press) + 2.0 * press
        press = (around + up(press) + down(press) - source) * SIXTH
    d_u = (-0.5 * step) * (walls.p_after(press) - walls.p_before(press))
    d_w = -step * (BETA * mean + 0.5 * (up(press) - down(press)))
    return d_u, d_w


def level_lanes(sums):
    spread = jnp.where(lanes() == levels(), jnp.broadcast_to(sums, (NZ, NX)), 0.0)
    return jnp.sum(spread, axis=0, keepdims=True)


def lane_means(row, start, width=1):
    low = levels() * width + start
    lane = lanes()
    spread = jnp.where((lane >= low) & (lane < low + width), jnp.broadcast_to(row, (NZ, NX)), 0.0)
    mean = jnp.sum(spread, axis=1, keepdims=True) * (1.0 / CELLS)
    return jnp.broadcast_to(mean, (NZ, NX))


def role_totals(rows, role):
    half = rows.shape[0] // 2
    pre = jnp.sum(rows[:half], axis=0, keepdims=True)
    suc = jnp.sum(rows[half:], axis=0, keepdims=True)
    return pre, jnp.where(role == 0, pre, suc)


def skewed(tiles):
    group = lanes(ROWS) // 8
    tiles = [tiles[-i % BLOCKS] for i in range(BLOCKS)]
    for bit in (1, 2, 4, 8):
        moved = (group & bit) != 0
        tiles = [jnp.where(moved, tiles[(i - bit) % BLOCKS], tiles[i]) for i in range(BLOCKS)]
    return tiles


def turned(tile, groups):
    shift = 8 * groups % NX
    return turn(tile, shift, 1) if shift else tile


def owner_of(block, flip):
    straight = block if block < 8 else 23 - block
    other = (8 if block == 0 else 16 - block) if block < 8 else (block - 7) % 8
    return jnp.where(flip == 0, straight, other)


def sampled(picked, f, r, cells, sample, base):
    shift = lax.rem(f * ROWS + r - sample[base + r] + 2 * NX, NX)
    return jnp.where(lanes() == f * ROWS + r, turn(cells, shift, 1), picked)


def with_gust(picked, level, base, rise):
    lane = lanes()
    for r in range(ROWS):
        gust = (1.5 + level[base + r].astype(jnp.float32)) * rise
        picked = picked + jnp.where(lane == r, gust, 0.0)
    return picked


def pack_kernel(info, began, state, mask, out, rises):
    role = info[0]
    flip = info[1]
    for section in range(3):
        span = jnp.full((1, NX), SECTION_T[section], jnp.float32) - began[0].astype(jnp.float32)
        angle = math.pi * jnp.clip(span / RISE, 0.0, 1.0)
        rises[section : section + 1] = 0.5 * (1.0 - jnp.cos(angle))
    for f in range(5):
        if f < 4:
            cells = state[f]
        else:
            cells = jnp.where(role == 1, CDRAG * mask[...].astype(jnp.float32), 0.0)
        flat = cells.T
        if f == 3:
            row = jnp.broadcast_to(jnp.sum(flat, axis=0, keepdims=True), (ROWS, NX))
            for block in range(BLOCKS):
                out[block, 5] = row
        flat = turn(flat, ROWS * info[2], 1)
        for block in range(BLOCKS):
            out[owner_of(block, flip), f] = flat[ROWS * block : ROWS * (block + 1)]


def first_kernel(info, sample, level, rises, chunks, buf, plane, sums_out):
    base = info[3]
    picked = jnp.zeros((NZ, NX), jnp.float32)
    sums = chunks[0, 5, :1]
    for s in range(1, BLOCKS):
        sums = sums + chunks[s, 5, :1]
    sums_out[...] = sums
    for f in range(5):
        tiles = skewed([chunks[s, f] for s in range(BLOCKS)])
        for z in range(NZ):
            buf[pl.ds(f * FIELD + z, ROWS, stride=NZ), :] = turned(tiles[z], -z)
    for f in range(4):
        for r in range(ROWS):
            spot = f * ROWS + r
            cells = buf[spot * NZ : (spot + 1) * NZ, :]
            picked = sampled(picked, f, r, cells, sample, base)
    picked = with_gust(picked, level, base, rises[:1])
    plane[...] = picked
    buf[5 * FIELD :, :] = picked


def section_kernel(section, info, *refs):
    refs = list(refs)

    def take(n):
        out = refs[:n]
        del refs[:n]
        return out

    if section < 2:
        sample, level, rises = take(3)
        base = info[3]
    starts = take(3)
    bufs = take(3) if section else starts
    if section:
        (sums_in,) = take(1)
    if section < 2:
        new_out, plane_out, sums_out = take(3)
    else:
        (chunks_out,) = take(1)
    ext, tent, press, src, face, natural = refs

    role = info[0]
    step = SECTION_C[section] * DT
    walls = Walls(role == 1)
    plane_at = (4 if section else 5) * FIELD

    if section:
        pre, own = role_totals(sums_in, role)
        spot = (0, 8) if section == 1 else (NZ, 1)
        prev_step = SECTION_C[section - 1] * DT
        d_u, d_w = mean_change(walls, lane_means(own, *spot), prev_step)
        _, pre_w = mean_change(Walls(role < 0), lane_means(pre, *spot), prev_step)

    if section == 2:
        changes = mean_change(walls, lane_means(own * 0.5, 0), step)
        now_u, now_w = (swap_blocks(change) for change in changes)
        row = lax.broadcasted_iota(jnp.int32, (ROWS, NX), 0)
        for s in range(BLOCKS):
            share = jnp.where(row == 0, now_u[s : s + 1], now_w[s : s + 1])
            chunks_out[s, 4] = share

    for side in range(3):
        plane = bufs[side][plane_at : plane_at + NZ, :]
        for r in range(ROWS):
            j = side * ROWS + r
            for f in range(4):
                at = (f * ROWS + r) * NZ
                cells = bufs[side][at : at + NZ, :]
                shift = (NX - (f * ROWS + r)) % NX
                ghost = turn(plane, shift, 1) if shift else plane
                if section and f == 0:
                    cells = cells + d_u
                if section and f == 2:
                    cells = cells + d_w
                    ghost = ghost + pre_w
                ext[f, j] = cells
                face[f, j] = ghost

    def rate_row(side, r):
        j = side * ROWS + r
        mid = [ext[f, j] for f in range(3)]
        nxt = [ext[f, j + 1] for f in range(3)]
        prv = [ext[f, j - 1] for f in range(3)]
        after = [walls.after(m) for m in mid]
        before = [walls.before(mid[f], face[f, j]) for f in range(3)]
        hi = [up(mid[0]), up(mid[1]), up(mid[2], 0.0)]
        lo = [down(mid[0]), down(mid[1]), down(mid[2], 0.0)]
        u, v, w = mid
        g_x = [(after[f] - before[f]) * 0.5 for f in range(3)]
        g_y = [(nxt[f] - prv[f]) * 0.5 for f in range(3)]
        g_z = [(hi[f] - lo[f]) * 0.5 for f in range(3)]
        a = g_y[0] + g_x[1]
        b = g_z[0] + g_x[2]
        e = g_z[1] + g_y[2]
        strain = g_x[0] * g_x[0] + g_y[1] * g_y[1] + g_z[2] * g_z[2] + 0.5 * (a * a + b * b + e * e)
        nu = SMAG * jnp.sqrt(2.0 * strain + EPS)
        at = pl.multiple_of(DRAG_AT + r * NZ, NZ)
        resist = starts[side][pl.ds(at, NZ), :] * jnp.sqrt(u * u + v * v + EPS)
        rates = []
        for f in range(3):
            lap = after[f] + before[f] + nxt[f] + prv[f] + hi[f] + lo[f] - 6.0 * mid[f]
            rates.append(nu * lap - (u * g_x[f] + v * g_y[f] + w * g_z[f]))
        rates[0] = rates[0] - resist * u
        rates[1] = rates[1] - resist * v
        theta = ext[3, j]
        rates[2] = rates[2] + BETA * theta
        for f in range(3):
            at = pl.multiple_of((f * ROWS + r) * NZ, NZ)
            tent[f, j] = starts[side][pl.ds(at, NZ), :] + step * rates[f]
        return u, v, w, nu, theta

    def heat_row(r, u, v, w, nu, mid):
        j = ROWS + r
        nxt = ext[3, j + 1]
        prv = ext[3, j - 1]
        after = walls.after(mid)
        before = walls.before(mid, face[3, j])
        hi = up(mid)
        lo = down(mid)
        g_x = (after - before) * 0.5
        g_y = (nxt - prv) * 0.5
        g_z = (hi - lo) * 0.5
        lap = after + before + nxt + prv + hi + lo - 6.0 * mid
        rate = PRINV * nu * lap - (u * g_x + v * g_y + w * g_z)
        at = pl.multiple_of((3 * ROWS + r) * NZ, NZ)
        tent[3, j] = starts[1][pl.ds(at, NZ), :] + step * rate

    def outer(side, r, carry):
        rate_row(side, r)
        return carry

    def inner(r, carry):
        heat_row(r, *rate_row(1, r))
        return carry

    lax.fori_loop(1, ROWS, functools.partial(outer, 0), 0, unroll=True)
    lax.fori_loop(0, ROWS, inner, 0, unroll=True)
    lax.fori_loop(0, ROWS - 1, functools.partial(outer, 2), 0, unroll=True)

    for j in range(2, EXT - 2):
        u = tent[0, j]
        w = tent[2, j]
        div = walls.after(u) - walls.before(u, face[0, j])
        div = div + (tent[1, j + 1] - tent[1, j - 1]) + (up(w, 0.0) - down(w, 0.0))
        scaled = div * (0.5 * SIXTH / step)
        src[j] = scaled
        press[0, j] = -scaled
    for sweep in range(1, SWEEPS):
        old = press.at[(sweep - 1) % 2]
        new = press.at[sweep % 2]
        for j in range(2 + sweep, EXT - 2 - sweep):
            mid = old[j]
            total = walls.p_after(mid) + walls.p_before(mid) + old[j + 1] + old[j - 1]
            total = total + up(mid) + down(mid)
            new[j] = total * SIXTH - src[j]
    final = press.at[(SWEEPS - 1) % 2]

    picked = jnp.zeros((NZ, NX), jnp.float32)
    sums = jnp.zeros((NZ, NX), jnp.float32)
    half = 0.5 * step
    for r in range(ROWS):
        j = ROWS + r
        mid = final[j]
        fresh = (
            tent[0, j] - half * (walls.p_after(mid) - walls.p_before(mid)),
            tent[1, j] - half * (final[j + 1] - final[j - 1]),
            tent[2, j] - half * (up(mid) - down(mid)),
            tent[3, j],
        )
        for f in range(4):
            spot = f * ROWS + r
            if section < 2:
                new_out[spot * NZ : (spot + 1) * NZ, :] = fresh[f]
                picked = sampled(picked, f, r, fresh[f], sample, base)
            else:
                natural[pl.ds(f * FIELD + r, NZ, stride=ROWS), :] = fresh[f]
        sums = sums + fresh[3]
    if section < 2:
        picked = with_gust(picked, level, base, rises[section + 1 : section + 2])
        new_out[plane_at if section else 4 * FIELD :, :] = picked
        plane_out[...] = picked
        sums_out[...] = level_lanes(jnp.sum(sums, axis=1, keepdims=True))
    else:
        for f in range(4):
            tiles = []
            for z in range(NZ):
                at = f * FIELD + z * ROWS
                tiles.append(turned(natural[at : at + ROWS, :], z))
            tiles = skewed(tiles)
            for s in range(BLOCKS):
                chunks_out[s, f] = tiles[s]


def last_kernel(info, chunks, out, held, left):
    flip = info[1]
    gx = info[2]
    share = chunks[0, 4]
    for block in range(1, BLOCKS):
        share = share + chunks[block, 4]
    shift = lax.rem(NX - ROWS * gx, NX)
    copies = [pltpu.make_async_copy(held.at[f], out.at[f], left.at[f]) for f in range(4)]
    for f in range(4):
        flat = jnp.concatenate([chunks[owner_of(block, flip), f] for block in range(BLOCKS)])
        flat = turn(flat, shift, 1)
        if f in (0, 2):
            flat = flat + share[f // 2 : f // 2 + 1]
        held[f] = flat.T
        copies[f].start()
    for copy in copies:
        copy.wait()


VMEM = pl.BlockSpec(memory_space=pltpu.VMEM)
SMEM = pl.BlockSpec(memory_space=pltpu.SMEM)
HBM = pl.BlockSpec(memory_space=pltpu.HBM)


def shape(*dims):
    return jax.ShapeDtypeStruct(dims, jnp.float32)


def call(body, name, small, args, outs, scratch=(), in_place=(VMEM, VMEM)):
    return pl.pallas_call(
        body,
        name=name,
        out_shape=outs,
        in_specs=[SMEM] * len(small) + [in_place[0]] * len(args),
        out_specs=[in_place[1]] * len(outs),
        scratch_shapes=list(scratch),
        compiler_params=pltpu.CompilerParams(vmem_limit_bytes=48 * 1024 * 1024),
    )(*small, *args)


def section_call(section, small, args):
    if section < 2:
        outs = [shape(4 * FIELD + NZ, NX), shape(NZ, NX), shape(1, NX)]
    else:
        outs = [shape(BLOCKS, 5, ROWS, NX)]
    row = (NZ, NX)
    scratch = [(4, EXT), (4, EXT), (2, EXT), (EXT,), (4, EXT)]
    scratch = [pltpu.VMEM((*lead, *row), jnp.float32) for lead in scratch]
    scratch.append(pltpu.VMEM((4 * FIELD, NX), jnp.float32))
    body = functools.partial(section_kernel, section)
    return call(body, f"section{section}", small, args, outs, scratch)


def ring_order():
    order = []
    for gy in range(8):
        even = [*range(8), *range(15, 7, -1)]
        odd = [8, *range(15, 8, -1), *range(1, 8), 0]
        order += [gx * 8 + gy for gx in (odd if gy % 2 else even)]
    return order


def around(cells, distance):
    order = ring_order()
    route = [(d, order[(i + distance) % len(order)]) for i, d in enumerate(order)]
    return lax.ppermute(cells, ("gx", "gy"), route)


def inflow_to(buf, plane):
    plane = lax.ppermute(plane, "role", [(0, 1)])
    return lax.dynamic_update_slice(buf, plane, (buf.shape[0] - NZ, 0))


def halo(buf):
    return around(buf, 1), buf, around(buf, -1)


def every(row, axes, count):
    return lax.all_to_all(jnp.broadcast_to(row[None], (count, 1, NX)), axes, 0, 0)[:, 0]


def along_z(row):
    groups = [list(range(8)), list(range(8, 16))]
    rows = jnp.broadcast_to(row[None], (8, 1, NX))
    return lax.all_to_all(rows, "gx", 0, 0, axis_index_groups=groups)[:, 0]


def across_z(row):
    high = [(role * 16 + half * 8) * 8 for role in range(2) for half in range(2)]
    groups = [[h + z * 8 + gy for h in high for gy in range(8)] for z in range(8)]
    rows = jnp.broadcast_to(row[None], (32, 1, NX))
    return lax.all_to_all(rows, ("role", "gx", "gy"), 0, 0, axis_index_groups=groups)[:, 0]


def per_device(state, turbine_mask, sample_x, gust_start, gust_level):
    role = lax.axis_index("role")
    gx = lax.axis_index("gx")
    flip = lax.axis_index("gy") % 2
    even = jnp.where(gx < 8, gx, 23 - gx)
    odd = jnp.where(gx < 8, 8 + (gx + 7) % 8, jnp.where(gx == 8, 0, 16 - gx))
    block = jnp.where(flip == 0, even, odd)
    info = jnp.stack([role, flip, gx, block * ROWS]).astype(jnp.int32)
    args = (state.reshape(4, 128, 128), turbine_mask.reshape(128, 128))
    outs = [shape(BLOCKS, 6, ROWS, NX), shape(3, NX)]
    chunks, rises = call(pack_kernel, "pack", (info, gust_start), args, outs)
    chunks, rises = lax.optimization_barrier((chunks, rises))
    inlet = (info, sample_x, gust_level)
    chunks = lax.all_to_all(chunks, "gx", 0, 0)
    outs = [shape(5 * FIELD + NZ, NX), shape(NZ, NX), shape(1, NX)]
    args = (rises, chunks)
    buf, plane, sums = call(first_kernel, "first", inlet, args, outs)
    starts = halo(inflow_to(buf, plane))
    totals = every(sums, ("role", "gy"), 16)
    buf, plane, sums = section_call(0, inlet, (rises, *starts))
    plane, totals = lax.optimization_barrier((plane, totals))
    bufs = halo(inflow_to(buf, plane))
    rows = along_z(sums)
    buf, plane, sums = section_call(1, inlet, (rises, *starts, *bufs, totals))
    plane, rows = lax.optimization_barrier((plane, rows))
    bufs = halo(inflow_to(buf, plane))
    row = jnp.sum(rows, axis=0, keepdims=True)
    row = jnp.concatenate([sums[:, :NZ], row[:, : NX - NZ]], axis=1)
    totals = across_z(row)
    (chunks,) = section_call(2, (info,), (*starts, *bufs, totals))
    chunks = lax.all_to_all(chunks, "gx", 0, 0)
    scratch = [pltpu.VMEM((4, 128, 128), jnp.float32), pltpu.SemaphoreType.DMA((4,))]
    outs = [shape(4, 128, 128)]
    (out,) = call(last_kernel, "last", (info,), (chunks,), outs, scratch, (VMEM, HBM))
    return out.reshape(1, 4, NZ, 8, 128)


def solution(mesh):
    placed = (P("role", None, None, "gx", "gy"), P(None, "gx", "gy"), P("gy"), P(), P("gy"))
    return jax.shard_map(
        per_device,
        mesh=mesh,
        in_specs=placed,
        out_specs=P("role", None, None, "gx", "gy"),
        check_vma=False,
    )
```

```python
import functools
import math

import jax
import jax.numpy as jnp
from jax import lax
from jax.experimental import pallas as pl
from jax.experimental.pallas import tpu as pltpu
from jax.sharding import PartitionSpec as P

SWEEPS = 6
DT = 0.25
SMAG = 0.1
BETA = 0.5
PRINV = 3.0
CDRAG = 1.0
RISE = 40.0
EPS = 1e-06
SECTION_C = (1.0 / 3.0, 0.5, 1.0)
SECTION_T = (0.0, 1.0 / 3.0, 0.5)

NZ = 16
NX = 128
ROWS = 8
EXT = 3 * ROWS
BLOCKS = 16
CELLS = 131072.0
SIXTH = 1.0 / 6.0
FIELD = ROWS * NZ
DRAG_AT = 4 * FIELD


def lanes(rows=NZ):
    return lax.broadcasted_iota(jnp.int32, (rows, NX), 1)


def levels():
    return lax.broadcasted_iota(jnp.int32, (NZ, NX), 0)


def turn(v, shift, axis):
    return pltpu.roll(v, shift, axis=axis)


def up(v, ghost=None):
    low, high = v[:8], v[8:]
    edge = lax.broadcasted_iota(jnp.int32, (8, NX), 0) == 7
    low_up, high_up = turn(low, 7, 0), turn(high, 7, 0)
    top = jnp.where(edge, high if ghost is None else ghost, high_up)
    return jnp.concatenate([jnp.where(edge, high_up, low_up), top])


def down(v, ghost=None):
    low, high = v[:8], v[8:]
    edge = lax.broadcasted_iota(jnp.int32, (8, NX), 0) == 0
    low_down, high_down = turn(low, 1, 0), turn(high, 1, 0)
    base = jnp.where(edge, low if ghost is None else ghost, low_down)
    return jnp.concatenate([base, jnp.where(edge, low_down, high_down)])


def swap_blocks(v):
    row = levels()
    group = lanes() // 8
    for bit in (8, 4, 2, 1):
        row_set = (row & bit) != 0
        group_set = (group & bit) != 0
        from_low = turn(turn(v, NZ - bit, 0), 8 * bit, 1)
        from_high = turn(turn(v, bit, 0), NX - 8 * bit, 1)
        v = jnp.where(row_set == group_set, v, jnp.where(row_set, from_high, from_low))
    return v


class Walls:
    def __init__(self, walled):
        lane = lanes()
        limit = jnp.where(walled, NX, -NX)
        self.first = lane == limit - NX
        self.last = lane == limit - 1

    def after(self, v):
        return jnp.where(self.last, v, turn(v, NX - 1, 1))

    def before(self, v, ghost):
        return jnp.where(self.first, ghost, turn(v, 1, 1))

    def p_after(self, v):
        return jnp.where(self.last, 0.0, turn(v, NX - 1, 1))

    def p_before(self, v):
        return jnp.where(self.first, 0.0, turn(v, 1, 1))


def mean_change(walls, mean, step):
    source = -0.5 * BETA * (up(mean, 0.0) - down(mean, 0.0))
    press = -SIXTH * source
    for _ in range(SWEEPS - 1):
        around = walls.p_after(press) + walls.p_before(press) + 2.0 * press
        press = (around + up(press) + down(press) - source) * SIXTH
    d_u = (-0.5 * step) * (walls.p_after(press) - walls.p_before(press))
    d_w = -step * (BETA * mean + 0.5 * (up(press) - down(press)))
    return d_u, d_w


def level_lanes(sums):
    spread = jnp.where(lanes() == levels(), jnp.broadcast_to(sums, (NZ, NX)), 0.0)
    return jnp.sum(spread, axis=0, keepdims=True)


def lane_means(row, start, width=1):
    low = levels() * width + start
    lane = lanes()
    spread = jnp.where((lane >= low) & (lane < low + width), jnp.broadcast_to(row, (NZ, NX)), 0.0)
    mean = jnp.sum(spread, axis=1, keepdims=True) * (1.0 / CELLS)
    return jnp.broadcast_to(mean, (NZ, NX))


def role_totals(rows, role):
    half = rows.shape[0] // 2
    pre = jnp.sum(rows[:half], axis=0, keepdims=True)
    suc = jnp.sum(rows[half:], axis=0, keepdims=True)
    return pre, jnp.where(role == 0, pre, suc)


def skewed(tiles):
    group = lanes(ROWS) // 8
    tiles = [tiles[-i % BLOCKS] for i in range(BLOCKS)]
    for bit in (1, 2, 4, 8):
        moved = (group & bit) != 0
        tiles = [jnp.where(moved, tiles[(i - bit) % BLOCKS], tiles[i]) for i in range(BLOCKS)]
    return tiles


def turned(tile, groups):
    shift = 8 * groups % NX
    return turn(tile, shift, 1) if shift else tile


def owner_of(block, flip):
    straight = block if block < 8 else 23 - block
    other = (8 if block == 0 else 16 - block) if block < 8 else (block - 7) % 8
    return jnp.where(flip == 0, straight, other)


def sampled(picked, f, r, cells, sample, base):
    shift = lax.rem(f * ROWS + r - sample[base + r] + 2 * NX, NX)
    return jnp.where(lanes() == f * ROWS + r, turn(cells, shift, 1), picked)


def with_gust(picked, level, base, rise):
    lane = lanes()
    for r in range(ROWS):
        gust = (1.5 + level[base + r].astype(jnp.float32)) * rise
        picked = picked + jnp.where(lane == r, gust, 0.0)
    return picked


def pack_kernel(info, began, state, mask, out, rises):
    role = info[0]
    flip = info[1]
    for section in range(3):
        span = jnp.full((1, NX), SECTION_T[section], jnp.float32) - began[0].astype(jnp.float32)
        angle = math.pi * jnp.clip(span / RISE, 0.0, 1.0)
        rises[section : section + 1] = 0.5 * (1.0 - jnp.cos(angle))
    for f in range(5):
        if f < 4:
            cells = state[f]
        else:
            cells = jnp.where(role == 1, CDRAG * mask[...].astype(jnp.float32), 0.0)
        flat = cells.T
        if f == 3:
            row = jnp.broadcast_to(jnp.sum(flat, axis=0, keepdims=True), (ROWS, NX))
            for block in range(BLOCKS):
                out[block, 5] = row
        flat = turn(flat, ROWS * info[2], 1)
        for block in range(BLOCKS):
            out[owner_of(block, flip), f] = flat[ROWS * block : ROWS * (block + 1)]


def first_kernel(info, sample, level, rises, chunks, buf, plane, sums_out):
    base = info[3]
    picked = jnp.zeros((NZ, NX), jnp.float32)
    sums = chunks[0, 5, :1]
    for s in range(1, BLOCKS):
        sums = sums + chunks[s, 5, :1]
    sums_out[...] = sums
    for f in range(5):
        tiles = skewed([chunks[s, f] for s in range(BLOCKS)])
        for z in range(NZ):
            buf[pl.ds(f * FIELD + z, ROWS, stride=NZ), :] = turned(tiles[z], -z)
    for f in range(4):
        for r in range(ROWS):
            spot = f * ROWS + r
            cells = buf[spot * NZ : (spot + 1) * NZ, :]
            picked = sampled(picked, f, r, cells, sample, base)
    picked = with_gust(picked, level, base, rises[:1])
    plane[...] = picked
    buf[5 * FIELD :, :] = picked


def section_kernel(section, info, *refs):
    refs = list(refs)

    def take(n):
        out = refs[:n]
        del refs[:n]
        return out

    if section < 2:
        sample, level, rises = take(3)
        base = info[3]
    starts = take(3)
    bufs = take(3) if section else starts
    if section:
        (sums_in,) = take(1)
    if section < 2:
        new_out, plane_out, sums_out = take(3)
    else:
        (chunks_out,) = take(1)
    ext, tent, press, src, face, natural = refs

    role = info[0]
    step = SECTION_C[section] * DT
    walls = Walls(role == 1)
    plane_at = (4 if section else 5) * FIELD

    if section:
        pre, own = role_totals(sums_in, role)
        spot = (0, 8) if section == 1 else (NZ, 1)
        prev_step = SECTION_C[section - 1] * DT
        d_u, d_w = mean_change(walls, lane_means(own, *spot), prev_step)
        _, pre_w = mean_change(Walls(role < 0), lane_means(pre, *spot), prev_step)

    if section == 2:
        changes = mean_change(walls, lane_means(own * 0.5, 0), step)
        now_u, now_w = (swap_blocks(change) for change in changes)
        row = lax.broadcasted_iota(jnp.int32, (ROWS, NX), 0)
        for s in range(BLOCKS):
            share = jnp.where(row == 0, now_u[s : s + 1], now_w[s : s + 1])
            chunks_out[s, 4] = share

    for side in range(3):
        plane = bufs[side][plane_at : plane_at + NZ, :]
        for r in range(ROWS):
            j = side * ROWS + r
            for f in range(4):
                at = (f * ROWS + r) * NZ
                cells = bufs[side][at : at + NZ, :]
                shift = (NX - (f * ROWS + r)) % NX
                ghost = turn(plane, shift, 1) if shift else plane
                if section and f == 0:
                    cells = cells + d_u
                if section and f == 2:
                    cells = cells + d_w
                    ghost = ghost + pre_w
                ext[f, j] = cells
                face[f, j] = ghost

    def rate_row(side, r):
        j = side * ROWS + r
        mid = [ext[f, j] for f in range(3)]
        nxt = [ext[f, j + 1] for f in range(3)]
        prv = [ext[f, j - 1] for f in range(3)]
        after = [walls.after(m) for m in mid]
        before = [walls.before(mid[f], face[f, j]) for f in range(3)]
        hi = [up(mid[0]), up(mid[1]), up(mid[2], 0.0)]
        lo = [down(mid[0]), down(mid[1]), down(mid[2], 0.0)]
        u, v, w = mid
        g_x = [(after[f] - before[f]) * 0.5 for f in range(3)]
        g_y = [(nxt[f] - prv[f]) * 0.5 for f in range(3)]
        g_z = [(hi[f] - lo[f]) * 0.5 for f in range(3)]
        a = g_y[0] + g_x[1]
        b = g_z[0] + g_x[2]
        e = g_z[1] + g_y[2]
        strain = g_x[0] * g_x[0] + g_y[1] * g_y[1] + g_z[2] * g_z[2] + 0.5 * (a * a + b * b + e * e)
        nu = SMAG * jnp.sqrt(2.0 * strain + EPS)
        at = pl.multiple_of(DRAG_AT + r * NZ, NZ)
        resist = starts[side][pl.ds(at, NZ), :] * jnp.sqrt(u * u + v * v + EPS)
        rates = []
        for f in range(3):
            lap = after[f] + before[f] + nxt[f] + prv[f] + hi[f] + lo[f] - 6.0 * mid[f]
            rates.append(nu * lap - (u * g_x[f] + v * g_y[f] + w * g_z[f]))
        rates[0] = rates[0] - resist * u
        rates[1] = rates[1] - resist * v
        theta = ext[3, j]
        rates[2] = rates[2] + BETA * theta
        for f in range(3):
            at = pl.multiple_of((f * ROWS + r) * NZ, NZ)
            tent[f, j] = starts[side][pl.ds(at, NZ), :] + step * rates[f]
        return u, v, w, nu, theta

    def heat_row(r, u, v, w, nu, mid):
        j = ROWS + r
        nxt = ext[3, j + 1]
        prv = ext[3, j - 1]
        after = walls.after(mid)
        before = walls.before(mid, face[3, j])
        hi = up(mid)
        lo = down(mid)
        g_x = (after - before) * 0.5
        g_y = (nxt - prv) * 0.5
        g_z = (hi - lo) * 0.5
        lap = after + before + nxt + prv + hi + lo - 6.0 * mid
        rate = PRINV * nu * lap - (u * g_x + v * g_y + w * g_z)
        at = pl.multiple_of((3 * ROWS + r) * NZ, NZ)
        tent[3, j] = starts[1][pl.ds(at, NZ), :] + step * rate

    def outer(side, r, carry):
        rate_row(side, r)
        return carry

    def inner(r, carry):
        heat_row(r, *rate_row(1, r))
        return carry

    lax.fori_loop(1, ROWS, functools.partial(outer, 0), 0, unroll=True)
    lax.fori_loop(0, ROWS, inner, 0, unroll=True)
    lax.fori_loop(0, ROWS - 1, functools.partial(outer, 2), 0, unroll=True)

    for j in range(2, EXT - 2):
        u = tent[0, j]
        w = tent[2, j]
        div = walls.after(u) - walls.before(u, face[0, j])
        div = div + (tent[1, j + 1] - tent[1, j - 1]) + (up(w, 0.0) - down(w, 0.0))
        scaled = div * (0.5 * SIXTH / step)
        src[j] = scaled
        press[0, j] = -scaled
    for sweep in range(1, SWEEPS):
        old = press.at[(sweep - 1) % 2]
        new = press.at[sweep % 2]
        for j in range(2 + sweep, EXT - 2 - sweep):
            mid = old[j]
            total = walls.p_after(mid) + walls.p_before(mid) + old[j + 1] + old[j - 1]
            total = total + up(mid) + down(mid)
            new[j] = total * SIXTH - src[j]
    final = press.at[(SWEEPS - 1) % 2]

    picked = jnp.zeros((NZ, NX), jnp.float32)
    sums = jnp.zeros((NZ, NX), jnp.float32)
    half = 0.5 * step
    for r in range(ROWS):
        j = ROWS + r
        mid = final[j]
        fresh = (
            tent[0, j] - half * (walls.p_after(mid) - walls.p_before(mid)),
            tent[1, j] - half * (final[j + 1] - final[j - 1]),
            tent[2, j] - half * (up(mid) - down(mid)),
            tent[3, j],
        )
        for f in range(4):
            spot = f * ROWS + r
            if section < 2:
                new_out[spot * NZ : (spot + 1) * NZ, :] = fresh[f]
                picked = sampled(picked, f, r, fresh[f], sample, base)
            else:
                natural[pl.ds(f * FIELD + r, NZ, stride=ROWS), :] = fresh[f]
        sums = sums + fresh[3]
    if section < 2:
        picked = with_gust(picked, level, base, rises[section + 1 : section + 2])
        new_out[plane_at if section else 4 * FIELD :, :] = picked
        plane_out[...] = picked
        sums_out[...] = level_lanes(jnp.sum(sums, axis=1, keepdims=True))
    else:
        for f in range(4):
            tiles = []
            for z in range(NZ):
                at = f * FIELD + z * ROWS
                tiles.append(turned(natural[at : at + ROWS, :], z))
            tiles = skewed(tiles)
            for s in range(BLOCKS):
                chunks_out[s, f] = tiles[s]


def last_kernel(info, chunks, out, held, left):
    flip = info[1]
    gx = info[2]
    share = chunks[0, 4]
    for block in range(1, BLOCKS):
        share = share + chunks[block, 4]
    shift = lax.rem(NX - ROWS * gx, NX)
    copies = [pltpu.make_async_copy(held.at[f], out.at[f], left.at[f]) for f in range(4)]
    for f in range(4):
        flat = jnp.concatenate([chunks[owner_of(block, flip), f] for block in range(BLOCKS)])
        flat = turn(flat, shift, 1)
        if f in (0, 2):
            flat = flat + share[f // 2 : f // 2 + 1]
        held[f] = flat.T
        copies[f].start()
    for copy in copies:
        copy.wait()


VMEM = pl.BlockSpec(memory_space=pltpu.VMEM)
SMEM = pl.BlockSpec(memory_space=pltpu.SMEM)
HBM = pl.BlockSpec(memory_space=pltpu.HBM)


def shape(*dims):
    return jax.ShapeDtypeStruct(dims, jnp.float32)


def call(body, name, small, args, outs, scratch=(), in_place=(VMEM, VMEM)):
    return pl.pallas_call(
        body,
        name=name,
        out_shape=outs,
        in_specs=[SMEM] * len(small) + [in_place[0]] * len(args),
        out_specs=[in_place[1]] * len(outs),
        scratch_shapes=list(scratch),
        compiler_params=pltpu.CompilerParams(vmem_limit_bytes=48 * 1024 * 1024),
    )(*small, *args)


def section_call(section, small, args):
    if section < 2:
        outs = [shape(4 * FIELD + NZ, NX), shape(NZ, NX), shape(1, NX)]
    else:
        outs = [shape(BLOCKS, 5, ROWS, NX)]
    row = (NZ, NX)
    scratch = [(4, EXT), (4, EXT), (2, EXT), (EXT,), (4, EXT)]
    scratch = [pltpu.VMEM((*lead, *row), jnp.float32) for lead in scratch]
    scratch.append(pltpu.VMEM((4 * FIELD + ROWS, NX), jnp.float32))
    body = functools.partial(section_kernel, section)
    return call(body, f"section{section}", small, args, outs, scratch)


def ring_order():
    order = []
    for gy in range(8):
        even = [*range(8), *range(15, 7, -1)]
        odd = [8, *range(15, 8, -1), *range(1, 8), 0]
        order += [gx * 8 + gy for gx in (odd if gy % 2 else even)]
    return order


def around(cells, distance):
    order = ring_order()
    route = [(d, order[(i + distance) % len(order)]) for i, d in enumerate(order)]
    return lax.ppermute(cells, ("gx", "gy"), route)


def inflow_to(buf, plane):
    plane = lax.ppermute(plane, "role", [(0, 1)])
    return lax.dynamic_update_slice(buf, plane, (buf.shape[0] - NZ, 0))


def halo(buf):
    return around(buf, 1), buf, around(buf, -1)


def every(row, axes, count):
    return lax.all_to_all(jnp.broadcast_to(row[None], (count, 1, NX)), axes, 0, 0)[:, 0]


def along_z(row):
    groups = [list(range(8)), list(range(8, 16))]
    rows = jnp.broadcast_to(row[None], (8, 1, NX))
    return lax.all_to_all(rows, "gx", 0, 0, axis_index_groups=groups)[:, 0]


def across_z(row):
    high = [(role * 16 + half * 8) * 8 for role in range(2) for half in range(2)]
    groups = [[h + z * 8 + gy for h in high for gy in range(8)] for z in range(8)]
    rows = jnp.broadcast_to(row[None], (32, 1, NX))
    return lax.all_to_all(rows, ("role", "gx", "gy"), 0, 0, axis_index_groups=groups)[:, 0]


def per_device(state, turbine_mask, sample_x, gust_start, gust_level):
    role = lax.axis_index("role")
    gx = lax.axis_index("gx")
    flip = lax.axis_index("gy") % 2
    even = jnp.where(gx < 8, gx, 23 - gx)
    odd = jnp.where(gx < 8, 8 + (gx + 7) % 8, jnp.where(gx == 8, 0, 16 - gx))
    block = jnp.where(flip == 0, even, odd)
    info = jnp.stack([role, flip, gx, block * ROWS]).astype(jnp.int32)
    args = (state.reshape(4, 128, 128), turbine_mask.reshape(128, 128))
    outs = [shape(BLOCKS, 6, ROWS, NX), shape(3, NX)]
    chunks, rises = call(pack_kernel, "pack", (info, gust_start), args, outs)
    chunks, rises = lax.optimization_barrier((chunks, rises))
    inlet = (info, sample_x, gust_level)
    chunks = lax.all_to_all(chunks, "gx", 0, 0)
    outs = [shape(5 * FIELD + NZ, NX), shape(NZ, NX), shape(1, NX)]
    args = (rises, chunks)
    buf, plane, sums = call(first_kernel, "first", inlet, args, outs)
    starts = halo(inflow_to(buf, plane))
    totals = every(sums, ("role", "gy"), 16)
    buf, plane, sums = section_call(0, inlet, (rises, *starts))
    plane, totals = lax.optimization_barrier((plane, totals))
    bufs = halo(inflow_to(buf, plane))
    rows = along_z(sums)
    buf, plane, sums = section_call(1, inlet, (rises, *starts, *bufs, totals))
    plane, rows = lax.optimization_barrier((plane, rows))
    bufs = halo(inflow_to(buf, plane))
    row = jnp.sum(rows, axis=0, keepdims=True)
    row = jnp.concatenate([sums[:, :NZ], row[:, : NX - NZ]], axis=1)
    totals = across_z(row)
    (chunks,) = section_call(2, (info,), (*starts, *bufs, totals))
    chunks = lax.all_to_all(chunks, "gx", 0, 0)
    scratch = [pltpu.VMEM((4, 128, 128), jnp.float32), pltpu.SemaphoreType.DMA((4,))]
    outs = [shape(4, 128, 128)]
    (out,) = call(last_kernel, "last", (info,), (chunks,), outs, scratch, (VMEM, HBM))
    return out.reshape(1, 4, NZ, 8, 128)


def solution(mesh):
    placed = (P("role", None, None, "gx", "gy"), P(None, "gx", "gy"), P("gy"), P(), P("gy"))
    return jax.shard_map(
        per_device,
        mesh=mesh,
        in_specs=placed,
        out_specs=P("role", None, None, "gx", "gy"),
        check_vma=False,
    )
```

```python
import functools
import math

import jax
import jax.numpy as jnp
from jax import lax
from jax.experimental import pallas as pl
from jax.experimental.pallas import tpu as pltpu
from jax.sharding import PartitionSpec as P

SWEEPS = 6
DT = 0.25
SMAG = 0.1
BETA = 0.5
PRINV = 3.0
CDRAG = 1.0
RISE = 40.0
EPS = 1e-06
SECTION_C = (1.0 / 3.0, 0.5, 1.0)
SECTION_T = (0.0, 1.0 / 3.0, 0.5)

NZ = 16
NX = 128
ROWS = 8
EXT = 3 * ROWS
BLOCKS = 16
CELLS = 131072.0
SIXTH = 1.0 / 6.0
FIELD = ROWS * NZ


def lanes(rows=NZ):
    return lax.broadcasted_iota(jnp.int32, (rows, NX), 1)


def levels():
    return lax.broadcasted_iota(jnp.int32, (NZ, NX), 0)


def turn(v, shift, axis):
    return pltpu.roll(v, shift, axis=axis)


def up(v, ghost=None):
    low, high = v[:8], v[8:]
    edge = lax.broadcasted_iota(jnp.int32, (8, NX), 0) == 7
    low_up, high_up = turn(low, 7, 0), turn(high, 7, 0)
    top = jnp.where(edge, high if ghost is None else ghost, high_up)
    return jnp.concatenate([jnp.where(edge, high_up, low_up), top])


def down(v, ghost=None):
    low, high = v[:8], v[8:]
    edge = lax.broadcasted_iota(jnp.int32, (8, NX), 0) == 0
    low_down, high_down = turn(low, 1, 0), turn(high, 1, 0)
    base = jnp.where(edge, low if ghost is None else ghost, low_down)
    return jnp.concatenate([base, jnp.where(edge, low_down, high_down)])


def swap_blocks(v):
    row = levels()
    group = lanes() // 8
    for bit in (8, 4, 2, 1):
        row_set = (row & bit) != 0
        group_set = (group & bit) != 0
        from_low = turn(turn(v, NZ - bit, 0), 8 * bit, 1)
        from_high = turn(turn(v, bit, 0), NX - 8 * bit, 1)
        v = jnp.where(row_set == group_set, v, jnp.where(row_set, from_high, from_low))
    return v


class Walls:
    def __init__(self, walled):
        lane = lanes()
        limit = jnp.where(walled, NX, -NX)
        self.first = lane == limit - NX
        self.last = lane == limit - 1

    def after(self, v):
        return jnp.where(self.last, v, turn(v, NX - 1, 1))

    def before(self, v, ghost):
        return jnp.where(self.first, ghost, turn(v, 1, 1))

    def p_after(self, v):
        return jnp.where(self.last, 0.0, turn(v, NX - 1, 1))

    def p_before(self, v):
        return jnp.where(self.first, 0.0, turn(v, 1, 1))


def mean_change(walls, mean, step):
    source = -0.5 * BETA * (up(mean, 0.0) - down(mean, 0.0))
    press = -SIXTH * source
    for _ in range(SWEEPS - 1):
        around = walls.p_after(press) + walls.p_before(press) + 2.0 * press
        press = (around + up(press) + down(press) - source) * SIXTH
    d_u = (-0.5 * step) * (walls.p_after(press) - walls.p_before(press))
    d_w = -step * (BETA * mean + 0.5 * (up(press) - down(press)))
    return d_u, d_w


def level_lanes(sums):
    spread = jnp.where(lanes() == levels(), jnp.broadcast_to(sums, (NZ, NX)), 0.0)
    return jnp.sum(spread, axis=0, keepdims=True)


def lane_means(row, start, width=1):
    low = levels() * width + start
    lane = lanes()
    spread = jnp.where((lane >= low) & (lane < low + width), jnp.broadcast_to(row, (NZ, NX)), 0.0)
    mean = jnp.sum(spread, axis=1, keepdims=True) * (1.0 / CELLS)
    return jnp.broadcast_to(mean, (NZ, NX))


def role_totals(rows, role):
    half = rows.shape[0] // 2
    pre = jnp.sum(rows[:half], axis=0, keepdims=True)
    suc = jnp.sum(rows[half:], axis=0, keepdims=True)
    return pre, jnp.where(role == 0, pre, suc)


def skewed(tiles):
    group = lanes(ROWS) // 8
    tiles = [tiles[-i % BLOCKS] for i in range(BLOCKS)]
    for bit in (1, 2, 4, 8):
        moved = (group & bit) != 0
        tiles = [jnp.where(moved, tiles[(i - bit) % BLOCKS], tiles[i]) for i in range(BLOCKS)]
    return tiles


def turned(tile, groups):
    shift = 8 * groups % NX
    return turn(tile, shift, 1) if shift else tile


def owner_of(block, flip):
    straight = block if block < 8 else 23 - block
    other = (8 if block == 0 else 16 - block) if block < 8 else (block - 7) % 8
    return jnp.where(flip == 0, straight, other)


def sampled(picked, f, r, cells, sample, base):
    shift = lax.rem(f * ROWS + r - sample[base + r] + 2 * NX, NX)
    return jnp.where(lanes() == f * ROWS + r, turn(cells, shift, 1), picked)


def with_gust(picked, level, base, rise):
    lane = lanes()
    for r in range(ROWS):
        gust = (1.5 + level[base + r].astype(jnp.float32)) * rise
        picked = picked + jnp.where(lane == r, gust, 0.0)
    return picked


def pack_kernel(info, began, state, mask, out, rises):
    role = info[0]
    flip = info[1]
    for section in range(3):
        span = jnp.full((1, NX), SECTION_T[section], jnp.float32) - began[0].astype(jnp.float32)
        angle = math.pi * jnp.clip(span / RISE, 0.0, 1.0)
        rises[section : section + 1] = 0.5 * (1.0 - jnp.cos(angle))
    for f in range(5):
        if f < 4:
            cells = state[f]
        else:
            cells = jnp.where(role == 1, CDRAG * mask[...].astype(jnp.float32), 0.0)
        flat = cells.T
        if f == 3:
            row = jnp.broadcast_to(jnp.sum(flat, axis=0, keepdims=True), (ROWS, NX))
            for block in range(BLOCKS):
                out[block, 5] = row
        flat = turn(flat, ROWS * info[2], 1)
        for block in range(BLOCKS):
            out[owner_of(block, flip), f] = flat[ROWS * block : ROWS * (block + 1)]


def first_kernel(info, sample, level, rises, chunks, buf, drag, plane, sums_out):
    base = info[3]
    picked = jnp.zeros((NZ, NX), jnp.float32)
    sums = chunks[0, 5, :1]
    for s in range(1, BLOCKS):
        sums = sums + chunks[s, 5, :1]
    sums_out[...] = sums
    for f in range(5):
        tiles = skewed([chunks[s, f] for s in range(BLOCKS)])
        for z in range(NZ):
            if f < 4:
                buf[pl.ds(f * FIELD + z, ROWS, stride=NZ), :] = turned(tiles[z], -z)
            else:
                drag[pl.ds(z, ROWS, stride=NZ), :] = turned(tiles[z], -z)
    for f in range(4):
        for r in range(ROWS):
            spot = f * ROWS + r
            cells = buf[spot * NZ : (spot + 1) * NZ, :]
            picked = sampled(picked, f, r, cells, sample, base)
    picked = with_gust(picked, level, base, rises[:1])
    plane[...] = picked
    buf[4 * FIELD :, :] = picked


def section_kernel(section, info, *refs):
    refs = list(refs)

    def take(n):
        out = refs[:n]
        del refs[:n]
        return out

    if section < 2:
        sample, level, rises = take(3)
        base = info[3]
    drags = take(3)
    starts = take(3)
    bufs = take(3) if section else starts
    if section:
        (sums_in,) = take(1)
    if section < 2:
        new_out, plane_out, sums_out = take(3)
    else:
        (chunks_out,) = take(1)
    ext, tent, press, src, face, natural = refs

    role = info[0]
    step = SECTION_C[section] * DT
    walls = Walls(role == 1)
    plane_at = 4 * FIELD

    if section:
        pre, own = role_totals(sums_in, role)
        spot = (0, 8) if section == 1 else (NZ, 1)
        prev_step = SECTION_C[section - 1] * DT
        d_u, d_w = mean_change(walls, lane_means(own, *spot), prev_step)
        _, pre_w = mean_change(Walls(role < 0), lane_means(pre, *spot), prev_step)

    if section == 2:
        changes = mean_change(walls, lane_means(own * 0.5, 0), step)
        now_u, now_w = (swap_blocks(change) for change in changes)
        row = lax.broadcasted_iota(jnp.int32, (ROWS, NX), 0)
        for s in range(BLOCKS):
            share = jnp.where(row == 0, now_u[s : s + 1], now_w[s : s + 1])
            chunks_out[s, 4] = share

    for side in range(3):
        plane = bufs[side][plane_at : plane_at + NZ, :]
        for r in range(ROWS):
            j = side * ROWS + r
            for f in range(4):
                at = (f * ROWS + r) * NZ
                cells = bufs[side][at : at + NZ, :]
                shift = (NX - (f * ROWS + r)) % NX
                ghost = turn(plane, shift, 1) if shift else plane
                if section and f == 0:
                    cells = cells + d_u
                if section and f == 2:
                    cells = cells + d_w
                    ghost = ghost + pre_w
                ext[f, j] = cells
                face[f, j] = ghost

    def rate_row(side, r):
        j = side * ROWS + r
        mid = [ext[f, j] for f in range(3)]
        nxt = [ext[f, j + 1] for f in range(3)]
        prv = [ext[f, j - 1] for f in range(3)]
        after = [walls.after(m) for m in mid]
        before = [walls.before(mid[f], face[f, j]) for f in range(3)]
        hi = [up(mid[0]), up(mid[1]), up(mid[2], 0.0)]
        lo = [down(mid[0]), down(mid[1]), down(mid[2], 0.0)]
        u, v, w = mid
        g_x = [(after[f] - before[f]) * 0.5 for f in range(3)]
        g_y = [(nxt[f] - prv[f]) * 0.5 for f in range(3)]
        g_z = [(hi[f] - lo[f]) * 0.5 for f in range(3)]
        a = g_y[0] + g_x[1]
        b = g_z[0] + g_x[2]
        e = g_z[1] + g_y[2]
        strain = g_x[0] * g_x[0] + g_y[1] * g_y[1] + g_z[2] * g_z[2] + 0.5 * (a * a + b * b + e * e)
        nu = SMAG * jnp.sqrt(2.0 * strain + EPS)
        at = pl.multiple_of(r * NZ, NZ)
        resist = drags[side][pl.ds(at, NZ), :] * jnp.sqrt(u * u + v * v + EPS)
        rates = []
        for f in range(3):
            lap = after[f] + before[f] + nxt[f] + prv[f] + hi[f] + lo[f] - 6.0 * mid[f]
            rates.append(nu * lap - (u * g_x[f] + v * g_y[f] + w * g_z[f]))
        rates[0] = rates[0] - resist * u
        rates[1] = rates[1] - resist * v
        theta = ext[3, j]
        rates[2] = rates[2] + BETA * theta
        for f in range(3):
            at = pl.multiple_of((f * ROWS + r) * NZ, NZ)
            tent[f, j] = starts[side][pl.ds(at, NZ), :] + step * rates[f]
        return u, v, w, nu, theta

    def heat_row(r, u, v, w, nu, mid):
        j = ROWS + r
        nxt = ext[3, j + 1]
        prv = ext[3, j - 1]
        after = walls.after(mid)
        before = walls.before(mid, face[3, j])
        hi = up(mid)
        lo = down(mid)
        g_x = (after - before) * 0.5
        g_y = (nxt - prv) * 0.5
        g_z = (hi - lo) * 0.5
        lap = after + before + nxt + prv + hi + lo - 6.0 * mid
        rate = PRINV * nu * lap - (u * g_x + v * g_y + w * g_z)
        at = pl.multiple_of((3 * ROWS + r) * NZ, NZ)
        tent[3, j] = starts[1][pl.ds(at, NZ), :] + step * rate

    def outer(side, r, carry):
        rate_row(side, r)
        return carry

    def inner(r, carry):
        heat_row(r, *rate_row(1, r))
        return carry

    lax.fori_loop(1, ROWS, functools.partial(outer, 0), 0, unroll=True)
    lax.fori_loop(0, ROWS, inner, 0, unroll=True)
    lax.fori_loop(0, ROWS - 1, functools.partial(outer, 2), 0, unroll=True)

    for j in range(2, EXT - 2):
        u = tent[0, j]
        w = tent[2, j]
        div = walls.after(u) - walls.before(u, face[0, j])
        div = div + (tent[1, j + 1] - tent[1, j - 1]) + (up(w, 0.0) - down(w, 0.0))
        scaled = div * (0.5 * SIXTH / step)
        src[j] = scaled
        press[0, j] = -scaled
    for sweep in range(1, SWEEPS):
        old = press.at[(sweep - 1) % 2]
        new = press.at[sweep % 2]
        for j in range(2 + sweep, EXT - 2 - sweep):
            mid = old[j]
            total = walls.p_after(mid) + walls.p_before(mid) + old[j + 1] + old[j - 1]
            total = total + up(mid) + down(mid)
            new[j] = total * SIXTH - src[j]
    final = press.at[(SWEEPS - 1) % 2]

    picked = jnp.zeros((NZ, NX), jnp.float32)
    sums = jnp.zeros((NZ, NX), jnp.float32)
    half = 0.5 * step
    for r in range(ROWS):
        j = ROWS + r
        mid = final[j]
        fresh = (
            tent[0, j] - half * (walls.p_after(mid) - walls.p_before(mid)),
            tent[1, j] - half * (final[j + 1] - final[j - 1]),
            tent[2, j] - half * (up(mid) - down(mid)),
            tent[3, j],
        )
        for f in range(4):
            spot = f * ROWS + r
            if section < 2:
                new_out[spot * NZ : (spot + 1) * NZ, :] = fresh[f]
                picked = sampled(picked, f, r, fresh[f], sample, base)
            else:
                natural[pl.ds(f * FIELD + r, NZ, stride=ROWS), :] = fresh[f]
        sums = sums + fresh[3]
    if section < 2:
        picked = with_gust(picked, level, base, rises[section + 1 : section + 2])
        new_out[plane_at if section else 4 * FIELD :, :] = picked
        plane_out[...] = picked
        sums_out[...] = level_lanes(jnp.sum(sums, axis=1, keepdims=True))
    else:
        for f in range(4):
            tiles = []
            for z in range(NZ):
                at = f * FIELD + z * ROWS
                tiles.append(turned(natural[at : at + ROWS, :], z))
            tiles = skewed(tiles)
            for s in range(BLOCKS):
                chunks_out[s, f] = tiles[s]


def last_kernel(info, chunks, out, held, left):
    flip = info[1]
    gx = info[2]
    share = chunks[0, 4]
    for block in range(1, BLOCKS):
        share = share + chunks[block, 4]
    shift = lax.rem(NX - ROWS * gx, NX)
    copies = [pltpu.make_async_copy(held.at[f], out.at[f], left.at[f]) for f in range(4)]
    for f in range(4):
        flat = jnp.concatenate([chunks[owner_of(block, flip), f] for block in range(BLOCKS)])
        flat = turn(flat, shift, 1)
        if f in (0, 2):
            flat = flat + share[f // 2 : f // 2 + 1]
        held[f] = flat.T
        copies[f].start()
    for copy in copies:
        copy.wait()


VMEM = pl.BlockSpec(memory_space=pltpu.VMEM)
SMEM = pl.BlockSpec(memory_space=pltpu.SMEM)
HBM = pl.BlockSpec(memory_space=pltpu.HBM)


def shape(*dims):
    return jax.ShapeDtypeStruct(dims, jnp.float32)


def call(body, name, small, args, outs, scratch=(), in_place=(VMEM, VMEM)):
    return pl.pallas_call(
        body,
        name=name,
        out_shape=outs,
        in_specs=[SMEM] * len(small) + [in_place[0]] * len(args),
        out_specs=[in_place[1]] * len(outs),
        scratch_shapes=list(scratch),
        compiler_params=pltpu.CompilerParams(vmem_limit_bytes=48 * 1024 * 1024),
    )(*small, *args)


def section_call(section, small, args):
    if section < 2:
        outs = [shape(4 * FIELD + NZ, NX), shape(NZ, NX), shape(1, NX)]
    else:
        outs = [shape(BLOCKS, 5, ROWS, NX)]
    row = (NZ, NX)
    scratch = [(4, EXT), (4, EXT), (2, EXT), (EXT,), (4, EXT)]
    scratch = [pltpu.VMEM((*lead, *row), jnp.float32) for lead in scratch]
    scratch.append(pltpu.VMEM((4 * FIELD + ROWS, NX), jnp.float32))
    body = functools.partial(section_kernel, section)
    return call(body, f"section{section}", small, args, outs, scratch)


def ring_order():
    order = []
    for gy in range(8):
        even = [*range(8), *range(15, 7, -1)]
        odd = [8, *range(15, 8, -1), *range(1, 8), 0]
        order += [gx * 8 + gy for gx in (odd if gy % 2 else even)]
    return order


def around(cells, distance):
    order = ring_order()
    route = [(d, order[(i + distance) % len(order)]) for i, d in enumerate(order)]
    return lax.ppermute(cells, ("gx", "gy"), route)


def farm_around(cells, distance):
    order = ring_order()
    route = [(128 + d, 128 + order[(i + distance) % 128]) for i, d in enumerate(order)]
    return lax.ppermute(cells, ("role", "gx", "gy"), route)


def inflow_to(buf, plane):
    plane = lax.ppermute(plane, "role", [(0, 1)])
    return lax.dynamic_update_slice(buf, plane, (buf.shape[0] - NZ, 0))


def halo(buf):
    return around(buf, 1), buf, around(buf, -1)


def every(row, axes, count):
    return lax.all_to_all(jnp.broadcast_to(row[None], (count, 1, NX)), axes, 0, 0)[:, 0]


def along_z(row):
    groups = [list(range(8)), list(range(8, 16))]
    rows = jnp.broadcast_to(row[None], (8, 1, NX))
    return lax.all_to_all(rows, "gx", 0, 0, axis_index_groups=groups)[:, 0]


def across_z(row):
    high = [(role * 16 + half * 8) * 8 for role in range(2) for half in range(2)]
    groups = [[h + z * 8 + gy for h in high for gy in range(8)] for z in range(8)]
    rows = jnp.broadcast_to(row[None], (32, 1, NX))
    return lax.all_to_all(rows, ("role", "gx", "gy"), 0, 0, axis_index_groups=groups)[:, 0]


def per_device(state, turbine_mask, sample_x, gust_start, gust_level):
    role = lax.axis_index("role")
    gx = lax.axis_index("gx")
    flip = lax.axis_index("gy") % 2
    even = jnp.where(gx < 8, gx, 23 - gx)
    odd = jnp.where(gx < 8, 8 + (gx + 7) % 8, jnp.where(gx == 8, 0, 16 - gx))
    block = jnp.where(flip == 0, even, odd)
    info = jnp.stack([role, flip, gx, block * ROWS]).astype(jnp.int32)
    args = (state.reshape(4, 128, 128), turbine_mask.reshape(128, 128))
    outs = [shape(BLOCKS, 6, ROWS, NX), shape(3, NX)]
    chunks, rises = call(pack_kernel, "pack", (info, gust_start), args, outs)
    chunks, rises = lax.optimization_barrier((chunks, rises))
    inlet = (info, sample_x, gust_level)
    chunks = lax.all_to_all(chunks, "gx", 0, 0)
    outs = [shape(4 * FIELD + NZ, NX), shape(FIELD + NZ, NX), shape(NZ, NX), shape(1, NX)]
    args = (rises, chunks)
    buf, drag, plane, sums = call(first_kernel, "first", inlet, args, outs)
    starts = halo(inflow_to(buf, plane))
    drags = (farm_around(drag, 1), drag, farm_around(drag, -1))
    totals = every(sums, ("role", "gy"), 16)
    buf, plane, sums = section_call(0, inlet, (rises, *drags, *starts))
    plane, totals = lax.optimization_barrier((plane, totals))
    bufs = halo(inflow_to(buf, plane))
    rows = along_z(sums)
    buf, plane, sums = section_call(1, inlet, (rises, *drags, *starts, *bufs, totals))
    plane, rows = lax.optimization_barrier((plane, rows))
    bufs = halo(inflow_to(buf, plane))
    row = jnp.sum(rows, axis=0, keepdims=True)
    row = jnp.concatenate([sums[:, :NZ], row[:, : NX - NZ]], axis=1)
    totals = across_z(row)
    (chunks,) = section_call(2, (info,), (*drags, *starts, *bufs, totals))
    chunks = lax.all_to_all(chunks, "gx", 0, 0)
    scratch = [pltpu.VMEM((4, 128, 128), jnp.float32), pltpu.SemaphoreType.DMA((4,))]
    outs = [shape(4, 128, 128)]
    (out,) = call(last_kernel, "last", (info,), (chunks,), outs, scratch, (VMEM, HBM))
    return out.reshape(1, 4, NZ, 8, 128)


def solution(mesh):
    placed = (P("role", None, None, "gx", "gy"), P(None, "gx", "gy"), P("gy"), P(), P("gy"))
    return jax.shard_map(
        per_device,
        mesh=mesh,
        in_specs=placed,
        out_specs=P("role", None, None, "gx", "gy"),
        check_vma=False,
    )
```
